256 devices in a mesh: fsdp: 8 (over z), expert: 32 (over x, y, core).
Axes of the slice: x: 4, y: 4, z: 8, core: 2. Of those that a mesh axis runs over, the one named last changes fastest.
Arguments:
- x_quant: bfloat16 [32768, 6144], P(('fsdp', 'expert')), may hold values from -6 to 6
- x_scale: float32 [32768, 48], P(('fsdp', 'expert')), may hold values from 0.3 to 3
- grad_out: bfloat16 [32768, 6144], P(('fsdp', 'expert')), may hold values from -6 to 6
- route_mask: int32 [32768], P(('fsdp', 'expert')), may hold values from 0 to 1, as said below
- route_prob: bfloat16 [32768], P(('fsdp', 'expert')), may hold values from 0.19921875 to 0.8984375
- gate_quant: bfloat16 [6144, 8192], P('fsdp', 'expert'), may hold values from -0.078125 to 0.078125
- gate_scale: float32 [48, 64], P('fsdp', 'expert'), may hold values from 0.5 to 2
- up_quant: bfloat16 [6144, 8192], P('fsdp', 'expert'), may hold values from -0.078125 to 0.078125
- up_scale: float32 [48, 64], P('fsdp', 'expert'), may hold values from 0.5 to 2
- down_quant: bfloat16 [8192, 6144], P('expert', 'fsdp'), may hold values from -0.0625 to 0.0625
- down_scale: float32 [64, 48], P('expert', 'fsdp'), may hold values from 0.5 to 2
Outputs:
- grad_x: bfloat16 [32768, 6144], P(('fsdp', 'expert'))
- grad_prob: float32 [32768], P(('fsdp', 'expert'))
- grad_gate: float32 [6144, 8192], P('fsdp', 'expert')
- grad_up: float32 [6144, 8192], P('fsdp', 'expert')
- grad_down: float32 [8192, 6144], P('expert', 'fsdp')
The draws below stay inside these ranges and needn't reach their ends.
Inputs may be any that keep to these rules, and one draw needn't show every extreme that they name: `route_mask`: each block of 128 consecutive tokens (the tokens of one device) has 1 to 8 routed tokens; in every draw there is a run of 32 consecutive blocks (one index of fsdp) in which every block has exactly 8.
All inputs are finite; a program needn't handle non-finite values.
Results may differ from the reference program's by a relative error of at most 0.015.
Values may be sent and summed in bfloat16 or wider, within the bound.
No kernel may reach another device: no remote copies, remote signals or barrier semaphores. Data moves between devices by JAX's collectives and lax.ppermute only.
A program may use at most 128 MiB of HBM per device.

```python
import math
import jax
import jax.numpy as jnp
from jax import lax

D = 6144
FF = 8192
QB = 128
TOK_DEV = 128
CAP = 8
TOKENS = 32768
N_EXPERT = 32


def draw_route_mask(key, part):
    key = jax.random.fold_in(key, 11)
    block_count = TOKENS // TOK_DEV
    group_count = block_count // N_EXPERT
    count_key, group_key, order_key = jax.random.split(key, 3)
    counts = jax.random.randint(count_key, (block_count,), 1, CAP + 1)
    full_group = jax.random.randint(group_key, (), 0, group_count)
    block_group = jnp.arange(block_count, dtype=jnp.int32) // N_EXPERT
    counts = jnp.where(block_group == full_group, CAP, counts)
    order_keys = jax.random.split(order_key, block_count)

    def shuffled(one_key):
        return jax.random.permutation(one_key, TOK_DEV)
    ranks = jax.vmap(shuffled)(order_keys)
    return (ranks < counts[:, None]).astype(jnp.int32).reshape(TOKENS)


def block_levels(stream_key, dims, cuts, smallest, high):
    gain = 1.0
    for position, parts in cuts:
        steps = jax.random.uniform(jax.random.fold_in(jax.random.fold_in(stream_key, 6), position), (parts,), jnp.float32, smallest / len(cuts), high / len(cuts))
        gain = gain * jnp.repeat(jnp.exp(steps), dims[position] // parts).reshape((-1,) + (1,) * (len(dims) - 1 - position))
    return gain


def bell_draw(own_key, dims, spread, limit, cuts=(), held_as=jnp.bfloat16):
    factor_of = block_levels(own_key, dims, cuts, -0.22, 0.18) if cuts else 1.0
    entries = jax.random.normal(own_key, dims, jnp.float32) * spread * factor_of
    return jnp.minimum(jnp.maximum(entries, -limit), limit).astype(held_as)


def setup_inputs(seed: int = 0) -> dict:
    seeds = jax.random.split(jax.random.key(seed), 12)
    return {
        "x_quant": bell_draw(seeds[0], (TOKENS, D), 1.0, 6.0, ((0, 256),)),
        "x_scale": jnp.clip(jnp.exp(math.log(3.0) - 2.3025851 * jax.random.uniform(seeds[1], (TOKENS, D // QB), jnp.float32) ** block_levels(seeds[1], (TOKENS, D // QB), ((0, 256),), -0.2, 0.2)), 0.3, 3.0),
        "grad_out": bell_draw(seeds[2], (TOKENS, D), 1.0, 6.0, ((0, 256),)),
        "route_mask": draw_route_mask(jax.random.fold_in(seeds[11], 71), 0),
        "route_prob": jnp.clip(0.19921875 + 0.69921875 * jax.random.uniform(seeds[4], (TOKENS,), jnp.float32) ** block_levels(seeds[4], (TOKENS,), ((0, 256),), -0.2, 0.2), 0.19921875, 0.8984375).astype(jnp.bfloat16),
        "gate_quant": bell_draw(seeds[5], (D, FF), D ** -0.5, 0.078125, ((0, 8), (1, 32))),
        "gate_scale": jnp.clip(jnp.exp(math.log(2.0) - 1.3862944 * jax.random.uniform(seeds[6], (D // QB, FF // QB), jnp.float32) ** block_levels(seeds[6], (D // QB, FF // QB), ((0, 8), (1, 32)), -0.2, 0.2)), 0.5, 2.0),
        "up_quant": bell_draw(seeds[7], (D, FF), D ** -0.5, 0.078125, ((0, 8), (1, 32))),
        "up_scale": jnp.clip(jnp.exp(math.log(2.0) - 1.3862944 * jax.random.uniform(seeds[8], (D // QB, FF // QB), jnp.float32) ** block_levels(seeds[8], (D // QB, FF // QB), ((0, 8), (1, 32)), -0.2, 0.2)), 0.5, 2.0),
        "down_quant": bell_draw(seeds[9], (FF, D), FF ** -0.5, 0.0625, ((0, 32), (1, 8))),
        "down_scale": jnp.clip(jnp.exp(math.log(2.0) - 1.3862944 * jax.random.uniform(seeds[10], (FF // QB, D // QB), jnp.float32) ** block_levels(seeds[10], (FF // QB, D // QB), ((0, 32), (1, 8)), -0.2, 0.2)), 0.5, 2.0),
    }


def scale_rows(quant, scales):
    rows, cols = quant.shape
    grouped = quant.astype(jnp.float32).reshape(rows, scales.shape[1], cols // scales.shape[1])
    return (grouped * scales[:, :, None]).reshape(rows, cols).astype(jnp.bfloat16)


def scale_tiles(quant, scales):
    rows, cols = quant.shape
    tall, broad = scales.shape
    grouped = quant.astype(jnp.float32).reshape(tall, rows // tall, broad, cols // broad)
    return (grouped * scales[:, None, :, None]).reshape(rows, cols).astype(jnp.bfloat16)


def contract(left, right, left_dim, right_dim):
    return lax.dot_general(left, right, (((left_dim,), (right_dim,)), ((), ())), preferred_element_type=jnp.float32)


def local_grads(gate_pre, up_pre, back_proj, slot_prob):
    sigmoid_gate = jax.nn.sigmoid(gate_pre)
    hidden = (gate_pre * sigmoid_gate * up_pre).astype(jnp.bfloat16)
    prob_part = jnp.sum(hidden.astype(jnp.float32) * back_proj, axis=1)
    grad_hidden = slot_prob * back_proj
    grad_up_act = (grad_hidden * gate_pre * sigmoid_gate).astype(jnp.bfloat16)
    grad_gate_act = (grad_hidden * up_pre * sigmoid_gate * (1.0 + gate_pre * (1.0 - sigmoid_gate))).astype(jnp.bfloat16)
    return hidden, prob_part, grad_gate_act, grad_up_act


def reference(x_quant, x_scale, grad_out, route_mask, route_prob, gate_quant, gate_scale, up_quant, up_scale, down_quant, down_scale):
    features = scale_rows(x_quant, x_scale)
    w_gate = scale_tiles(gate_quant, gate_scale)
    w_up = scale_tiles(up_quant, up_scale)
    w_down = scale_tiles(down_quant, down_scale)
    block_count = TOKENS // TOK_DEV
    mask_rows = route_mask.reshape(block_count, TOK_DEV)
    slot_rank = (jnp.cumsum(mask_rows, axis=1) - 1).astype(jnp.int32)
    slot_ids = jnp.arange(CAP, dtype=jnp.int32)
    table = ((slot_rank[:, None, :] == slot_ids[None, :, None]) & (mask_rows[:, None, :] == 1)).astype(jnp.float32)

    def to_slots(values):
        grouped = values.astype(jnp.float32).reshape(block_count, TOK_DEV, -1)
        placed = jnp.einsum("bct,btd->bcd", table, grouped, precision=lax.Precision.HIGHEST)
        return placed.reshape(block_count * CAP, -1)

    slot_x = to_slots(features).astype(jnp.bfloat16)
    slot_dy = to_slots(grad_out).astype(jnp.bfloat16)
    slot_prob = to_slots(route_prob.reshape(TOKENS, 1))
    weighted = (slot_prob * slot_dy.astype(jnp.float32)).astype(jnp.bfloat16)
    pieces = 8
    piece_width = FF // pieces

    def fold_step(carry, piece_index):
        grad_acc, prob_acc = carry
        col_start = piece_index * piece_width
        gate_cols = lax.dynamic_slice_in_dim(w_gate, col_start, piece_width, 1)
        up_cols = lax.dynamic_slice_in_dim(w_up, col_start, piece_width, 1)
        down_rows = lax.dynamic_slice_in_dim(w_down, col_start, piece_width, 0)
        gate_pre = jnp.dot(slot_x, gate_cols, preferred_element_type=jnp.float32)
        up_pre = jnp.dot(slot_x, up_cols, preferred_element_type=jnp.float32)
        back_proj = contract(slot_dy, down_rows, 1, 1)
        hidden, prob_part, grad_gate_act, grad_up_act = local_grads(gate_pre, up_pre, back_proj, slot_prob)
        grad_acc = grad_acc + contract(grad_gate_act, gate_cols, 1, 1) + contract(grad_up_act, up_cols, 1, 1)
        prob_acc = prob_acc + prob_part
        gate_piece = contract(slot_x, grad_gate_act, 0, 0)
        up_piece = contract(slot_x, grad_up_act, 0, 0)
        down_piece = contract(hidden, weighted, 0, 0)
        return (grad_acc, prob_acc), (gate_piece, up_piece, down_piece)

    start_acc = (jnp.zeros((block_count * CAP, D), jnp.float32), jnp.zeros((block_count * CAP,), jnp.float32))
    (slot_grad, slot_prob_grad), (gate_pieces, up_pieces, down_pieces) = lax.scan(fold_step, start_acc, jnp.arange(pieces, dtype=jnp.int32))
    grad_gate = jnp.transpose(gate_pieces, (1, 0, 2)).reshape(D, FF)
    grad_up = jnp.transpose(up_pieces, (1, 0, 2)).reshape(D, FF)
    grad_down = down_pieces.reshape(FF, D)
    grad_x = jnp.einsum("bct,bcd->btd", table, slot_grad.reshape(block_count, CAP, D), precision=lax.Precision.HIGHEST)
    grad_x = grad_x.reshape(TOKENS, D).astype(jnp.bfloat16)
    grad_prob = jnp.einsum("bct,bc->bt", table, slot_prob_grad.reshape(block_count, CAP), precision=lax.Precision.HIGHEST).reshape(TOKENS)
    return grad_x, grad_prob, grad_gate, grad_up, grad_down
```

```python
import jax
import jax.numpy as jnp
from jax import lax
from jax.sharding import Mesh
from jax.sharding import PartitionSpec as P

CAP = 8
PLANE = ("x", "y")
EXPERT = ("x", "y", "core")
BF16 = jnp.bfloat16
F32 = jnp.float32


def scale_tiles(quant, scales):
    rows, cols = quant.shape
    tall, broad = scales.shape
    grouped = quant.astype(F32).reshape(tall, rows // tall, broad, cols // broad)
    return (grouped * scales[:, None, :, None]).reshape(rows, cols).astype(BF16)


def contract(left, right, left_dim, right_dim):
    return lax.dot_general(
        left, right, (((left_dim,), (right_dim,)), ((), ())), preferred_element_type=F32
    )


def local_grads(gate_pre, up_pre, back_proj, slot_prob):
    sigmoid_gate = jax.nn.sigmoid(gate_pre)
    hidden = (gate_pre * sigmoid_gate * up_pre).astype(BF16)
    prob_part = jnp.sum(hidden.astype(F32) * back_proj, axis=1)
    grad_hidden = slot_prob * back_proj
    grad_up_act = (grad_hidden * gate_pre * sigmoid_gate).astype(BF16)
    grad_gate_act = (
        grad_hidden * up_pre * sigmoid_gate * (1.0 + gate_pre * (1.0 - sigmoid_gate))
    ).astype(BF16)
    return (hidden, prob_part, grad_gate_act, grad_up_act)


def turn(values, axis, place, size):
    flipped = jnp.flip(values, axis)
    twice = jnp.concatenate([flipped, flipped], axis)
    return lax.dynamic_slice_in_dim(twice, size - 1 - place, size, axis)


def ring_gather(block, axis, size, split):
    up = [(i, (i + 1) % size) for i in range(size)]
    down = [(i, (i - 1) % size) for i in range(size)]
    far = size // 2
    length = block.shape[split]
    pieces = [(0, 0, length, block)]
    ahead, behind = block, block
    for step in range(1, far):
        ahead = lax.ppermute(ahead, axis, up)
        behind = lax.ppermute(behind, axis, down)
        pieces.append((step, 0, length, ahead))
        pieces.append((size - step, 0, length, behind))
    half = length // 2
    ahead = lax.ppermute(lax.slice_in_dim(ahead, 0, half, axis=split), axis, up)
    behind = lax.ppermute(lax.slice_in_dim(behind, half, length, axis=split), axis, down)
    pieces.append((far, 0, half, ahead))
    pieces.append((far, half, length, behind))
    return pieces


def split_sum(values):
    high = values.astype(BF16)
    return jnp.stack([high, (values - high.astype(F32)).astype(BF16)], axis=-1)


def make_on_device(mesh):
    ring = mesh.shape["fsdp"]
    cores = mesh.shape["core"]

    def on_device(
        x_quant,
        x_scale,
        grad_out,
        route_mask,
        route_prob,
        gate_quant,
        gate_scale,
        up_quant,
        up_scale,
        down_quant,
        down_scale,
    ):
        place = lax.axis_index("fsdp")
        core = lax.axis_index("core")
        width = x_quant.shape[1]
        part = width // ring

        w_gate_up = jnp.concatenate(
            [scale_tiles(gate_quant, gate_scale), scale_tiles(up_quant, up_scale)], axis=1
        )
        w_down = scale_tiles(down_quant, down_scale)
        units = w_down.shape[0]
        gate_up_parts = ring_gather(w_gate_up, "fsdp", ring, 0)
        down_parts = ring_gather(w_down, "fsdp", ring, 1)

        slot_rank = jnp.cumsum(route_mask) - 1
        slot_ids = jnp.arange(CAP, dtype=jnp.int32)
        table = ((slot_rank[None, :] == slot_ids[:, None]) & (route_mask[None, :] == 1)).astype(BF16)
        table_wide = table.astype(F32)
        blocks = x_scale.shape[1]
        slot_quant = jnp.dot(table, x_quant, preferred_element_type=F32)
        slot_scale = jnp.dot(
            table_wide, x_scale, precision=lax.Precision.HIGHEST, preferred_element_type=F32
        )
        slot_x = (
            (slot_quant.reshape(CAP, blocks, width // blocks) * slot_scale[:, :, None])
            .reshape(CAP, width)
            .astype(BF16)
        )
        slot_dy = jnp.dot(table, grad_out, preferred_element_type=F32).astype(BF16)
        slot_prob = jnp.sum(table_wide * route_prob.astype(F32)[None, :], axis=1)
        weighted = (slot_prob[:, None] * slot_dy.astype(F32)).astype(BF16)

        turned = turn(
            jnp.stack([slot_x, slot_dy]).reshape(2, CAP, ring, part), 2, place, ring
        ).reshape(2, CAP, width)
        packed = jnp.concatenate(
            [turned[0], turned[1], jnp.broadcast_to(slot_prob.astype(BF16)[:, None], (CAP, 128))],
            axis=1,
        )
        rows = lax.all_gather(packed, EXPERT, axis=0, tiled=True)
        rows_x, rows_dy = rows[:, :width], rows[:, width : 2 * width]
        prob_col = rows[:, 2 * width : 2 * width + 1].astype(F32)

        sides = jnp.stack([slot_x.reshape(CAP, ring, part), weighted.reshape(CAP, ring, part)])
        sides = sides.transpose(2, 1, 0, 3).reshape(ring, CAP, 2 * part)
        sides = lax.all_to_all(sides, "fsdp", split_axis=0, concat_axis=0, tiled=True)
        sides = turn(sides, 0, place, ring)
        columns = lax.all_gather(sides, EXPERT, axis=1, tiled=True)

        gate_up_pre = sum(
            jnp.dot(
                rows_x[:, r * part + a : r * part + b], w, preferred_element_type=F32
            )
            for r, a, b, w in gate_up_parts
        )
        back_proj = sum(
            contract(rows_dy[:, r * part + a : r * part + b], w, 1, 1)
            for r, a, b, w in down_parts
        )
        hidden, prob_part, grad_gate_act, grad_up_act = local_grads(
            gate_up_pre[:, :units], gate_up_pre[:, units:], back_proj, prob_col
        )
        grad_acts = jnp.concatenate([grad_gate_act, grad_up_act], axis=1)
        act_parts = ring_gather(
            jnp.concatenate([grad_acts, hidden], axis=1), "fsdp", ring, 0
        )

        ordered = sorted(gate_up_parts, key=lambda piece: piece[:2])
        slot_grad = jnp.concatenate(
            [contract(grad_acts, w, 1, 1).astype(BF16) for _, _, _, w in ordered]
            + [jnp.pad(split_sum(prob_part), ((0, 0), (0, 126)))],
            axis=1,
        )
        wide = slot_grad.shape[1]
        slot_grad = slot_grad.reshape(-1, cores, CAP, wide)
        keep = lax.dynamic_index_in_dim(slot_grad, core, 1, keepdims=False)
        give = lax.dynamic_index_in_dim(slot_grad, 1 - core, 1, keepdims=False)
        got = lax.ppermute(give, "core", [(0, 1), (1, 0)])
        both = keep.astype(F32) + got.astype(F32)
        both = jnp.concatenate(
            [
                both[..., :width].astype(BF16),
                jnp.pad(
                    split_sum(both[..., width] + both[..., width + 1]), ((0, 0), (0, 0), (0, 126))
                ),
            ],
            axis=-1,
        )
        shares = lax.all_to_all(both, PLANE, split_axis=0, concat_axis=0, tiled=True)
        mine = jnp.sum(shares.astype(F32), axis=0)
        mine_grad = mine[:, :width].astype(BF16).reshape(CAP, ring, part)
        mine_grad = turn(mine_grad, 1, place, ring).reshape(CAP, width)
        mine_prob = mine[:, width] + mine[:, width + 1]
        grad_x = contract(table, mine_grad, 0, 0).astype(BF16)
        grad_prob = jnp.sum(table_wide * mine_prob[:, None], axis=0)

        grad_gate_up = sum(
            contract(columns[r, a:b, :part], acts[:, : 2 * units], 0, 0)
            for r, a, b, acts in act_parts
        )
        grad_down = sum(
            contract(acts[:, 2 * units :], columns[r, a:b, part:], 0, 0)
            for r, a, b, acts in act_parts
        )
        return (grad_x, grad_prob, grad_gate_up[:, :units], grad_gate_up[:, units:], grad_down)

    return on_device


def solution(mesh):
    devices = mesh.devices
    mesh = Mesh(devices.reshape(devices.shape[0], 4, 4, 2), ("fsdp", "x", "y", "core"))
    tokens = ("fsdp", "x", "y", "core")
    placed = (
        P(tokens, None),
        P(tokens, None),
        P(tokens, None),
        P(tokens),
        P(tokens),
        P("fsdp", EXPERT),
        P("fsdp", EXPERT),
        P("fsdp", EXPERT),
        P("fsdp", EXPERT),
        P(EXPERT, "fsdp"),
        P(EXPERT, "fsdp"),
    )
    return jax.shard_map(
        make_on_device(mesh),
        mesh=mesh,
        in_specs=placed,
        out_specs=(
            P(tokens, None),
            P(tokens),
            P("fsdp", EXPERT),
            P("fsdp", EXPERT),
            P(EXPERT, "fsdp"),
        ),
        check_vma=False,
    )
```

```python
import jax
import jax.numpy as jnp
from jax import lax
from jax.experimental import pallas as pl
from jax.experimental.pallas import tpu as pltpu
from jax.sharding import Mesh
from jax.sharding import PartitionSpec as P

CAP = 8
PLANE = ("x", "y")
EXPERT = ("x", "y", "core")
CORE_FIRST = ("core", "x", "y")
LANES = 128
BLOCK = 128
BF16 = jnp.bfloat16
F32 = jnp.float32


def contract(left, right, left_dim, right_dim):
    return lax.dot_general(
        left, right, (((left_dim,), (right_dim,)), ((), ())), preferred_element_type=F32
    )


def kernel_call(body, outs, limit, scalars=0, **specs):
    grid_spec = pltpu.PrefetchScalarGridSpec(num_scalar_prefetch=scalars, grid=(1,), **specs)
    return pl.pallas_call(
        body,
        out_shape=outs,
        grid_spec=grid_spec,
        compiler_params=pltpu.CompilerParams(vmem_limit_bytes=limit << 20),
    )


def whole(shape):
    return pl.BlockSpec(shape, lambda *_: (0,) * len(shape), pipeline_mode=pl.Buffered(1))


def block_at(shape, where):
    return pl.BlockSpec(shape, lambda *_: where, pipeline_mode=pl.Buffered(1))


def two_lanes(column):
    high = column.astype(BF16).astype(F32)
    lane = lax.broadcasted_iota(jnp.int32, (column.shape[0], LANES), 1)
    spread = jnp.where(lane == 0, high, jnp.where(lane == 1, column - high, 0.0))
    return spread.astype(BF16)


def scaled_weights(gate_quant, gate_scale, up_quant, up_scale, down_quant, down_scale):
    part, units = gate_quant.shape

    def put(out, quant, scale, shift):
        tall, broad = quant.shape[0] // BLOCK, quant.shape[1] // BLOCK
        for i in range(tall):
            for j in range(broad):
                rows, cols = slice(i * BLOCK, (i + 1) * BLOCK), slice(j * BLOCK, (j + 1) * BLOCK)
                out[rows, shift + j * BLOCK : shift + (j + 1) * BLOCK] = (
                    quant[rows, cols].astype(F32) * scale[i, j]
                ).astype(BF16)

    def body(gate, up, down, gate_s, up_s, down_s, gate_up_out, down_out):
        put(gate_up_out, gate, gate_s, 0)
        put(gate_up_out, up, up_s, units)
        put(down_out, down, down_s, 0)

    quants, scales = [gate_quant, up_quant, down_quant], [gate_scale, up_scale, down_scale]
    shapes = ((part, 2 * units), down_quant.shape)
    return kernel_call(
        body,
        tuple(jax.ShapeDtypeStruct(v, BF16) for v in shapes),
        16,
        in_specs=[whole(v.shape) for v in quants]
        + [pl.BlockSpec(memory_space=pltpu.SMEM)] * 3,
        out_specs=tuple(whole(v) for v in shapes),
    )(*quants, *scales)


def pre_sums(rows, gate_up_parts, down_parts):
    count = len(gate_up_parts)
    part, both = gate_up_parts[0][3].shape
    units = both // 2
    width = (rows.shape[1] - LANES) // 2
    places = [r for r, _, _, _ in gate_up_parts]
    assert places == [r for r, _, _, _ in down_parts]

    def body(rows_ref, *refs):
        out = refs[-1]
        pre = back = None
        for i, r in enumerate(places):
            x = rows_ref[:, r * part : (r + 1) * part]
            dy = rows_ref[:, width + r * part : width + (r + 1) * part]
            one = contract(x, refs[i][...], 1, 0)
            two = contract(dy, refs[count + i][...], 1, 1)
            pre = one if pre is None else pre + one
            back = two if back is None else back + two
        out[:, :both] = pre
        out[:, both:] = back

    weights = [p[3] for p in gate_up_parts] + [p[3] for p in down_parts]
    shape = (rows.shape[0], both + units)
    return kernel_call(
        body,
        jax.ShapeDtypeStruct(shape, F32),
        40,
        in_specs=[whole(v.shape) for v in [rows] + weights],
        out_specs=whole(shape),
    )(rows, *weights)


def activations(rows, sums, gate_up_parts, down_parts):
    count = rows.shape[0]
    both = gate_up_parts[0][3].shape[1]
    units = both // 2
    far = gate_up_parts[0][0]
    part = sum(b - a for _, a, b, _ in gate_up_parts)
    width = (rows.shape[1] - LANES) // 2

    def body(x_ref, dy_ref, prob_ref, sums_ref, wa, wb, da, db, acts_ref, prob_out):
        half = part // 2
        pre = sums_ref[:, :both]
        pre = pre + contract(x_ref[:, :half], wa[...], 1, 0)
        pre = pre + contract(x_ref[:, half:], wb[...], 1, 0)
        back = jnp.concatenate(
            [contract(dy_ref[...], da[...], 1, 1), contract(dy_ref[...], db[...], 1, 1)], axis=1
        )
        back = sums_ref[:, both:] + back
        gate_pre, up_pre = pre[:, :units], pre[:, units:]
        sigmoid_gate = jax.nn.sigmoid(gate_pre)
        hidden = (gate_pre * sigmoid_gate * up_pre).astype(BF16)
        prob_part = jnp.sum(hidden.astype(F32) * back, axis=1, keepdims=True)
        grad_hidden = prob_ref[:, :1].astype(F32) * back
        acts_ref[:, :units] = (
            grad_hidden * up_pre * sigmoid_gate * (1.0 + gate_pre * (1.0 - sigmoid_gate))
        ).astype(BF16)
        acts_ref[:, units:both] = (grad_hidden * gate_pre * sigmoid_gate).astype(BF16)
        acts_ref[:, both:] = hidden
        prob_out[...] = two_lanes(prob_part)

    weights = [p[3] for p in gate_up_parts] + [p[3] for p in down_parts]
    acts_shape, prob_shape = (count, both + units), (count, LANES)
    return kernel_call(
        body,
        (jax.ShapeDtypeStruct(acts_shape, BF16), jax.ShapeDtypeStruct(prob_shape, BF16)),
        32,
        in_specs=[
            block_at((count, part), (0, far)),
            block_at((count, part), (0, width // part + far)),
            block_at((count, LANES), (0, 2 * width // LANES)),
            whole(sums.shape),
        ]
        + [whole(v.shape) for v in weights],
        out_specs=(whole(acts_shape), whole(prob_shape)),
    )(rows, rows, rows, sums, *weights)


def slot_sums(core, acts, prob_lanes, gate_up_parts):
    half = acts.shape[0] // 2
    both = gate_up_parts[0][3].shape[1]
    part = gate_up_parts[0][2]
    width = sum(b - a for _, a, b, _ in gate_up_parts)
    places = [r * part + a for r, a, _, _ in gate_up_parts]

    def body(core_ref, acts_ref, prob_ref, *refs):
        for which, out in ((1 - core_ref[0], refs[-2]), (core_ref[0], refs[-1])):
            rows = pl.ds(pl.multiple_of(which * half, half), half)
            acts = acts_ref[rows, :both]
            for place, weight in zip(places, refs):
                out[:, place : place + weight.shape[0]] = contract(acts, weight[...], 1, 1).astype(
                    BF16
                )
            out[:, width:] = prob_ref[rows, :]

    weights = [p[3] for p in gate_up_parts]
    shape = (half, width + LANES)
    return kernel_call(
        body,
        (jax.ShapeDtypeStruct(shape, BF16),) * 2,
        40,
        scalars=1,
        in_specs=[whole(v.shape) for v in [acts, prob_lanes] + weights],
        out_specs=(whole(shape),) * 2,
    )(core, acts, prob_lanes, *weights)


def pair_sum(mine, other):
    width = mine.shape[1] - LANES

    def body(a_ref, b_ref, out):
        for at in range(0, width, 768):
            cols = slice(at, at + 768)
            out[:, cols] = (a_ref[:, cols].astype(F32) + b_ref[:, cols].astype(F32)).astype(BF16)
        lanes = a_ref[:, width:].astype(F32) + b_ref[:, width:].astype(F32)
        out[:, width:] = two_lanes(lanes[:, 0:1] + lanes[:, 1:2])

    return kernel_call(
        body,
        jax.ShapeDtypeStruct(mine.shape, BF16),
        16,
        in_specs=[whole(mine.shape)] * 2,
        out_specs=whole(mine.shape),
    )(mine, other)


def weight_sums(columns, act_parts):
    _, count, twice = columns.shape
    part = twice // 2
    wide = act_parts[0][3].shape[1]
    units = wide // 3
    places = [r for r, _, _, _ in act_parts]

    def body(cols_ref, *refs):
        gate_up = down = None
        for r, acts in zip(places, refs):
            one = contract(cols_ref[r, :, :part], acts[:, : 2 * units], 0, 0)
            two = contract(acts[:, 2 * units :], cols_ref[r, :, part:], 0, 0)
            gate_up = one if gate_up is None else gate_up + one
            down = two if down is None else down + two
        refs[-2][...] = gate_up
        refs[-1][...] = down

    shapes = ((part, 2 * units), (units, part))
    acts = [p[3] for p in act_parts]
    return kernel_call(
        body,
        tuple(jax.ShapeDtypeStruct(v, F32) for v in shapes),
        40,
        in_specs=[whole(v.shape) for v in [columns] + acts],
        out_specs=tuple(whole(v) for v in shapes),
    )(columns, *acts)


def last_weight_sums(columns, gate_up, down, act_parts):
    _, count, twice = columns.shape
    part = twice // 2
    units = down.shape[0]
    far = act_parts[0][0]

    def body(cols_ref, gate_up_ref, down_ref, aa, ab, gate_out, up_out, down_out):
        half = count // 2
        one, two = gate_up_ref[...], down_ref[...]
        for acts, rows in ((aa, slice(0, half)), (ab, slice(half, count))):
            one = one + contract(cols_ref[0, rows, :part], acts[:, : 2 * units], 0, 0)
            two = two + contract(acts[:, 2 * units :], cols_ref[0, rows, part:], 0, 0)
        gate_out[...] = one[:, :units]
        up_out[...] = one[:, units:]
        down_out[...] = two

    acts = [p[3] for p in act_parts]
    shapes = ((part, units), (part, units), (units, part))
    return kernel_call(
        body,
        tuple(jax.ShapeDtypeStruct(v, F32) for v in shapes),
        32,
        in_specs=[block_at((1, count, twice), (far, 0, 0))]
        + [whole(v.shape) for v in [gate_up, down] + acts],
        out_specs=tuple(whole(v) for v in shapes),
    )(columns, gate_up, down, *acts)


def turn(values, axis, place, size):
    flipped = jnp.flip(values, axis)
    twice = jnp.concatenate([flipped, flipped], axis)
    return lax.dynamic_slice_in_dim(twice, size - 1 - place, size, axis)


def ring_gather(block, axis, size):
    up = [(i, (i + 1) % size) for i in range(size)]
    down = [(i, (i - 1) % size) for i in range(size)]
    far = size // 2
    length = block.shape[0]
    near = [(0, 0, length, block)]
    ahead, behind = block, block
    for step in range(1, far):
        ahead = lax.ppermute(ahead, axis, up)
        behind = lax.ppermute(behind, axis, down)
        near.append((step, 0, length, ahead))
        near.append((size - step, 0, length, behind))
    half = length // 2
    ahead = lax.ppermute(ahead[:half], axis, up)
    behind = lax.ppermute(behind[half:], axis, down)
    return near, [(far, 0, half, ahead), (far, half, length, behind)]


def make_on_device(mesh):
    ring = mesh.shape["fsdp"]

    def on_device(
        x_quant,
        x_scale,
        grad_out,
        route_mask,
        route_prob,
        gate_quant,
        gate_scale,
        up_quant,
        up_scale,
        down_quant,
        down_scale,
    ):
        place = lax.axis_index("fsdp")
        core = lax.axis_index("core")
        width = x_quant.shape[1]
        part = width // ring

        w_gate_up, w_down = scaled_weights(
            gate_quant, gate_scale, up_quant, up_scale, down_quant, down_scale
        )
        down_near, down_far = ring_gather(w_down, "fsdp", ring)
        gate_up_near, gate_up_far = ring_gather(w_gate_up, "fsdp", ring)

        slot_rank = jnp.cumsum(route_mask) - 1
        slot_ids = jnp.arange(CAP, dtype=jnp.int32)
        table = ((slot_rank[None, :] == slot_ids[:, None]) & (route_mask[None, :] == 1)).astype(BF16)
        table_wide = table.astype(F32)
        blocks = x_scale.shape[1]
        slot_quant = jnp.dot(table, x_quant, preferred_element_type=F32)
        slot_scale = jnp.dot(
            table_wide, x_scale, precision=lax.Precision.HIGHEST, preferred_element_type=F32
        )
        slot_x = (
            (slot_quant.reshape(CAP, blocks, width // blocks) * slot_scale[:, :, None])
            .reshape(CAP, width)
            .astype(BF16)
        )
        slot_dy = jnp.dot(table, grad_out, preferred_element_type=F32).astype(BF16)
        slot_prob = jnp.sum(table_wide * route_prob.astype(F32)[None, :], axis=1)
        weighted = (slot_prob[:, None] * slot_dy.astype(F32)).astype(BF16)

        sides = jnp.concatenate(
            [slot_x.reshape(CAP, ring, part), weighted.reshape(CAP, ring, part)], axis=-1
        ).transpose(1, 0, 2)
        turned = turn(
            jnp.stack([slot_x, slot_dy]).reshape(2, CAP, ring, part), 2, place, ring
        ).reshape(2, CAP, width)
        packed = jnp.concatenate(
            [turned[0], turned[1], jnp.broadcast_to(slot_prob.astype(BF16)[:, None], (CAP, 128))],
            axis=1,
        )
        rows = lax.all_gather(packed, CORE_FIRST, axis=0, tiled=True)

        sides = lax.all_to_all(sides, "fsdp", split_axis=0, concat_axis=0, tiled=True)
        sides = turn(sides, 0, place, ring)
        columns = lax.all_gather(sides, CORE_FIRST, axis=1, tiled=True)

        sums = pre_sums(rows, gate_up_near, down_near)
        acts, prob_lanes = activations(rows, sums, gate_up_far, down_far)
        acts_near, acts_far = ring_gather(acts, "fsdp", ring)

        give, keep = slot_sums(core[None], acts, prob_lanes, gate_up_near + gate_up_far)
        got = lax.ppermute(give, "core", [(0, 1), (1, 0)])
        got, *_ = lax.optimization_barrier((got, acts_near[1][3], acts_near[2][3]))
        both = pair_sum(keep, got).reshape(-1, CAP, width + LANES)
        shares = lax.all_to_all(both, PLANE, split_axis=0, concat_axis=0, tiled=True)
        mine = jnp.sum(shares.astype(F32), axis=0)
        mine_grad = mine[:, :width].astype(BF16).reshape(CAP, ring, part)
        mine_grad = turn(mine_grad, 1, place, ring).reshape(CAP, width)
        mine_prob = mine[:, width] + mine[:, width + 1]
        grad_x = contract(table, mine_grad, 0, 0).astype(BF16)
        grad_prob = jnp.sum(table_wide * mine_prob[:, None], axis=0)

        gate_up, down = weight_sums(columns, acts_near)
        grad_gate, grad_up, grad_down = last_weight_sums(columns, gate_up, down, acts_far)
        return (grad_x, grad_prob, grad_gate, grad_up, grad_down)

    return on_device


def solution(mesh):
    devices = mesh.devices
    mesh = Mesh(devices.reshape(devices.shape[0], 4, 4, 2), ("fsdp", "x", "y", "core"))
    tokens = ("fsdp", "x", "y", "core")
    placed = (
        P(tokens, None),
        P(tokens, None),
        P(tokens, None),
        P(tokens),
        P(tokens),
        P("fsdp", EXPERT),
        P("fsdp", EXPERT),
        P("fsdp", EXPERT),
        P("fsdp", EXPERT),
        P(EXPERT, "fsdp"),
        P(EXPERT, "fsdp"),
    )
    return jax.shard_map(
        make_on_device(mesh),
        mesh=mesh,
        in_specs=placed,
        out_specs=(
            P(tokens, None),
            P(tokens),
            P("fsdp", EXPERT),
            P("fsdp", EXPERT),
            P(EXPERT, "fsdp"),
        ),
        check_vma=False,
    )
```

```python
import jax
import jax.numpy as jnp
from jax import lax
from jax.experimental import pallas as pl
from jax.experimental.pallas import tpu as pltpu
from jax.sharding import Mesh
from jax.sharding import PartitionSpec as P

CAP = 8
PLANE = ("x", "y")
EXPERT = ("x", "y", "core")
CORE_FIRST = ("core", "x", "y")
LANES = 128
BLOCK = 128
BF16 = jnp.bfloat16
F32 = jnp.float32


def contract(left, right, left_dim, right_dim):
    return lax.dot_general(
        left, right, (((left_dim,), (right_dim,)), ((), ())), preferred_element_type=F32
    )


def kernel_call(body, outs, limit, scalars=0, grid=(1,), **specs):
    grid_spec = pltpu.PrefetchScalarGridSpec(num_scalar_prefetch=scalars, grid=grid, **specs)
    return pl.pallas_call(
        body,
        out_shape=outs,
        grid_spec=grid_spec,
        compiler_params=pltpu.CompilerParams(vmem_limit_bytes=limit << 20),
    )


def far_memory():
    return pl.BlockSpec(memory_space=pl.ANY)


def whole(shape):
    return pl.BlockSpec(shape, lambda *_: (0,) * len(shape), pipeline_mode=pl.Buffered(1))


def block_at(shape, where):
    return pl.BlockSpec(shape, lambda *_: where, pipeline_mode=pl.Buffered(1))


def two_lanes(column):
    high = column.astype(BF16).astype(F32)
    lane = lax.broadcasted_iota(jnp.int32, (column.shape[0], LANES), 1)
    spread = jnp.where(lane == 0, high, jnp.where(lane == 1, column - high, 0.0))
    return spread.astype(BF16)


def scaled_weights(gate_quant, gate_scale, up_quant, up_scale, down_quant, down_scale):
    part, units = gate_quant.shape

    def put(out, quant, scale, shift):
        tall, broad = quant.shape[0] // BLOCK, quant.shape[1] // BLOCK
        for i in range(tall):
            for j in range(broad):
                rows, cols = slice(i * BLOCK, (i + 1) * BLOCK), slice(j * BLOCK, (j + 1) * BLOCK)
                out[rows, shift + j * BLOCK : shift + (j + 1) * BLOCK] = (
                    quant[rows, cols].astype(F32) * scale[i, j]
                ).astype(BF16)

    def body(gate, up, down, gate_s, up_s, down_s, gate_up_out, down_out):
        put(gate_up_out, gate, gate_s, 0)
        put(gate_up_out, up, up_s, units)
        put(down_out, down, down_s, 0)

    quants, scales = [gate_quant, up_quant, down_quant], [gate_scale, up_scale, down_scale]
    shapes = ((part, 2 * units), down_quant.shape)
    return kernel_call(
        body,
        tuple(jax.ShapeDtypeStruct(v, BF16) for v in shapes),
        60,
        in_specs=[whole(v.shape) for v in quants]
        + [pl.BlockSpec(memory_space=pltpu.SMEM)] * 3,
        out_specs=tuple(whole(v) for v in shapes),
    )(*quants, *scales)


def pre_sums(rows, gate_up_parts, down_parts):
    count = len(gate_up_parts)
    part, both = gate_up_parts[0][1].shape
    units = both // 2
    slots = rows.shape[0]
    width = (rows.shape[1] - LANES) // 2
    places = [r for r, _ in gate_up_parts]
    assert places == [r for r, _ in down_parts]

    def body(rows_ref, *refs):
        weights, out = refs[: 2 * count], refs[2 * count]
        x_in, dy_in, gate_up_in, down_in, sems = refs[2 * count + 1 :]
        copies = []
        for i, r in enumerate(places):
            copies.append(
                [
                    pltpu.make_async_copy(source, into.at[i], sems.at[k, i])
                    for k, (source, into) in enumerate(
                        (
                            (rows_ref.at[:, pl.ds(r * part, part)], x_in),
                            (rows_ref.at[:, pl.ds(width + r * part, part)], dy_in),
                            (weights[i], gate_up_in),
                            (weights[count + i], down_in),
                        )
                    )
                ]
            )
            for copy in copies[-1]:
                copy.start()
        pre = back = None
        for i in range(count):
            for copy in copies[i]:
                copy.wait()
            one = contract(x_in[i], gate_up_in[i], 1, 0)
            two = contract(dy_in[i], down_in[i], 1, 1)
            pre = one if pre is None else pre + one
            back = two if back is None else back + two
        out[:, :both] = pre
        out[:, both:] = back

    weights = [w for _, w in gate_up_parts] + [w for _, w in down_parts]
    shape = (slots, both + units)
    return kernel_call(
        body,
        jax.ShapeDtypeStruct(shape, F32),
        60,
        in_specs=[far_memory()] * (1 + 2 * count),
        out_specs=whole(shape),
        scratch_shapes=[
            pltpu.VMEM((count, slots, part), BF16),
            pltpu.VMEM((count, slots, part), BF16),
            pltpu.VMEM((count, part, both), BF16),
            pltpu.VMEM((count, units, part), BF16),
            pltpu.SemaphoreType.DMA((4, count)),
        ],
    )(rows, *weights)


def activations(rows, sums, gate_up_part, down_part):
    count = rows.shape[0]
    far, w_gate_up = gate_up_part
    w_down = down_part[1]
    part, both = w_gate_up.shape
    units = both // 2
    width = (rows.shape[1] - LANES) // 2

    def body(x_ref, dy_ref, prob_ref, sums_ref, gate_up_ref, down_ref, acts_ref, prob_out):
        pre = sums_ref[:, :both] + contract(x_ref[...], gate_up_ref[...], 1, 0)
        back = sums_ref[:, both:] + contract(dy_ref[...], down_ref[...], 1, 1)
        gate_pre, up_pre = pre[:, :units], pre[:, units:]
        sigmoid_gate = jax.nn.sigmoid(gate_pre)
        hidden = (gate_pre * sigmoid_gate * up_pre).astype(BF16)
        prob_part = jnp.sum(hidden.astype(F32) * back, axis=1, keepdims=True)
        grad_hidden = prob_ref[:, :1].astype(F32) * back
        acts_ref[:, :units] = (
            grad_hidden * up_pre * sigmoid_gate * (1.0 + gate_pre * (1.0 - sigmoid_gate))
        ).astype(BF16)
        acts_ref[:, units:both] = (grad_hidden * gate_pre * sigmoid_gate).astype(BF16)
        acts_ref[:, both:] = hidden
        prob_out[...] = two_lanes(prob_part)

    acts_shape, prob_shape = (count, both + units), (count, LANES)
    return kernel_call(
        body,
        (jax.ShapeDtypeStruct(acts_shape, BF16), jax.ShapeDtypeStruct(prob_shape, BF16)),
        60,
        in_specs=[
            block_at((count, part), (0, far)),
            block_at((count, part), (0, width // part + far)),
            block_at((count, LANES), (0, 2 * width // LANES)),
            whole(sums.shape),
            whole(w_gate_up.shape),
            whole(w_down.shape),
        ],
        out_specs=(whole(acts_shape), whole(prob_shape)),
    )(rows, rows, rows, sums, w_gate_up, w_down)


def slot_sums(core, acts, prob_lanes, gate_up_parts):
    half = acts.shape[0] // 2
    count = len(gate_up_parts)
    part, both = gate_up_parts[0][1].shape
    width = count * part
    places = [r for r, _ in gate_up_parts]

    def body(core_ref, acts_ref, prob_ref, *refs):
        weights, give, keep, weights_in, sems = refs[:count], *refs[count:]
        copies = [
            pltpu.make_async_copy(weights[i], weights_in.at[i], sems.at[i]) for i in range(count)
        ]
        for copy in copies:
            copy.start()
        theirs = pl.ds(pl.multiple_of((1 - core_ref[0]) * half, half), half)
        mine = pl.ds(pl.multiple_of(core_ref[0] * half, half), half)
        acts = jnp.concatenate([acts_ref[theirs, :both], acts_ref[mine, :both]], axis=0)
        for i, r in enumerate(places):
            copies[i].wait()
            sums = contract(acts, weights_in[i], 1, 1).astype(BF16)
            give[:, r * part : (r + 1) * part] = sums[:half]
            keep[:, r * part : (r + 1) * part] = sums[half:]
        give[:, width:] = prob_ref[theirs, :]
        keep[:, width:] = prob_ref[mine, :]

    weights = [w for _, w in gate_up_parts]
    shape = (half, width + LANES)
    return kernel_call(
        body,
        (jax.ShapeDtypeStruct(shape, BF16),) * 2,
        60,
        scalars=1,
        in_specs=[whole(acts.shape), whole(prob_lanes.shape)] + [far_memory()] * count,
        out_specs=(whole(shape),) * 2,
        scratch_shapes=[
            pltpu.VMEM((count, part, both), BF16),
            pltpu.SemaphoreType.DMA((count,)),
        ],
    )(core, acts, prob_lanes, *weights)


def pair_sum(mine, other):
    width = mine.shape[1] - LANES

    def body(a_ref, b_ref, out):
        for at in range(0, width, 768):
            cols = slice(at, at + 768)
            out[:, cols] = (a_ref[:, cols].astype(F32) + b_ref[:, cols].astype(F32)).astype(BF16)
        lanes = a_ref[:, width:].astype(F32) + b_ref[:, width:].astype(F32)
        out[:, width:] = two_lanes(lanes[:, 0:1] + lanes[:, 1:2])

    return kernel_call(
        body,
        jax.ShapeDtypeStruct(mine.shape, BF16),
        16,
        in_specs=[whole(mine.shape)] * 2,
        out_specs=whole(mine.shape),
    )(mine, other)


def weight_sums(columns, acts):
    slots, twice = columns.shape
    part, units = twice // 2, acts.shape[1] // 3
    tile = 256
    steps = part // tile

    def body(x_ref, weighted_ref, acts_ref, gate_out, up_out, down_out):
        both = contract(x_ref[...], acts_ref[:, : 2 * units], 0, 0)
        gate_out[...] = both[:, :units]
        up_out[...] = both[:, units:]
        down_out[...] = contract(acts_ref[:, 2 * units :], weighted_ref[...], 0, 0)

    return kernel_call(
        body,
        (
            jax.ShapeDtypeStruct((part, units), F32),
            jax.ShapeDtypeStruct((part, units), F32),
            jax.ShapeDtypeStruct((units, part), F32),
        ),
        60,
        grid=(steps,),
        in_specs=[
            pl.BlockSpec((slots, tile), lambda i: (0, i)),
            pl.BlockSpec((slots, tile), lambda i: (0, steps + i)),
            whole(acts.shape),
        ],
        out_specs=(
            pl.BlockSpec((tile, units), lambda i: (i, 0)),
            pl.BlockSpec((tile, units), lambda i: (i, 0)),
            pl.BlockSpec((units, tile), lambda i: (0, i)),
        ),
    )(columns, columns, acts)


def turn(values, axis, place, size):
    flipped = jnp.flip(values, axis)
    twice = jnp.concatenate([flipped, flipped], axis)
    return lax.dynamic_slice_in_dim(twice, size - 1 - place, size, axis)


def ring_gather(block, axis, size, last_up):
    up = [(i, (i + 1) % size) for i in range(size)]
    down = [(i, (i - 1) % size) for i in range(size)]
    far = size // 2
    parts = [(0, block)]
    ahead, behind = block, block
    for step in range(1, far):
        ahead = lax.ppermute(ahead, axis, up)
        behind = lax.ppermute(behind, axis, down)
        parts += [(step, ahead), (size - step, behind)]
    last = lax.ppermute(ahead, axis, up) if last_up else lax.ppermute(behind, axis, down)
    return parts, (far, last)


def make_on_device(mesh):
    ring = mesh.shape["fsdp"]

    def on_device(
        x_quant,
        x_scale,
        grad_out,
        route_mask,
        route_prob,
        gate_quant,
        gate_scale,
        up_quant,
        up_scale,
        down_quant,
        down_scale,
    ):
        place = lax.axis_index("fsdp")
        core = lax.axis_index("core")
        width = x_quant.shape[1]
        part = width // ring

        w_gate_up, w_down = scaled_weights(
            gate_quant, gate_scale, up_quant, up_scale, down_quant, down_scale
        )
        down_near, down_far = ring_gather(w_down, "fsdp", ring, False)
        gate_up_near, gate_up_far = ring_gather(w_gate_up, "fsdp", ring, True)

        slot_rank = jnp.cumsum(route_mask) - 1
        slot_ids = jnp.arange(CAP, dtype=jnp.int32)
        table = ((slot_rank[None, :] == slot_ids[:, None]) & (route_mask[None, :] == 1)).astype(BF16)
        table_wide = table.astype(F32)
        blocks = x_scale.shape[1]
        slot_quant = jnp.dot(table, x_quant, preferred_element_type=F32)
        slot_scale = jnp.dot(
            table_wide, x_scale, precision=lax.Precision.HIGHEST, preferred_element_type=F32
        )
        slot_x = (
            (slot_quant.reshape(CAP, blocks, width // blocks) * slot_scale[:, :, None])
            .reshape(CAP, width)
            .astype(BF16)
        )
        slot_dy = jnp.dot(table, grad_out, preferred_element_type=F32).astype(BF16)
        slot_prob = jnp.sum(table_wide * route_prob.astype(F32)[None, :], axis=1)
        weighted = (slot_prob[:, None] * slot_dy.astype(F32)).astype(BF16)

        sides = jnp.concatenate(
            [slot_x.reshape(CAP, ring, part), weighted.reshape(CAP, ring, part)], axis=-1
        ).transpose(1, 0, 2)
        turned = turn(
            jnp.stack([slot_x, slot_dy]).reshape(2, CAP, ring, part), 2, place, ring
        ).reshape(2, CAP, width)
        packed = jnp.concatenate(
            [turned[0], turned[1], jnp.broadcast_to(slot_prob.astype(BF16)[:, None], (CAP, 128))],
            axis=1,
        )
        rows = lax.all_gather(packed, CORE_FIRST, axis=0, tiled=True)

        sides = lax.all_to_all(sides, "fsdp", split_axis=0, concat_axis=0, tiled=True)
        columns = lax.all_gather(sides, CORE_FIRST, axis=1, tiled=True).reshape(-1, 2 * part)

        sums = pre_sums(rows, gate_up_near, down_near)
        acts, prob_lanes = activations(rows, sums, gate_up_far, down_far)
        all_acts = lax.all_gather(acts, "fsdp", axis=0, tiled=True)

        give, keep = slot_sums(core[None], acts, prob_lanes, [*gate_up_near, gate_up_far])
        got = lax.ppermute(give, "core", [(0, 1), (1, 0)])
        both = pair_sum(keep, got).reshape(-1, CAP, width + LANES)
        shares = lax.all_to_all(both, PLANE, split_axis=0, concat_axis=0, tiled=True)
        mine = jnp.sum(shares.astype(F32), axis=0)
        mine_grad = mine[:, :width].astype(BF16).reshape(CAP, ring, part)
        mine_grad = turn(mine_grad, 1, place, ring).reshape(CAP, width)
        mine_prob = mine[:, width] + mine[:, width + 1]
        grad_x = contract(table, mine_grad, 0, 0).astype(BF16)
        grad_prob = jnp.sum(table_wide * mine_prob[:, None], axis=0)

        grad_gate, grad_up, grad_down = weight_sums(columns, all_acts)
        return (grad_x, grad_prob, grad_gate, grad_up, grad_down)

    return on_device


def solution(mesh):
    devices = mesh.devices
    mesh = Mesh(devices.reshape(devices.shape[0], 4, 4, 2), ("fsdp", "x", "y", "core"))
    tokens = ("fsdp", "x", "y", "core")
    placed = (
        P(tokens, None),
        P(tokens, None),
        P(tokens, None),
        P(tokens),
        P(tokens),
        P("fsdp", EXPERT),
        P("fsdp", EXPERT),
        P("fsdp", EXPERT),
        P("fsdp", EXPERT),
        P(EXPERT, "fsdp"),
        P(EXPERT, "fsdp"),
    )
    return jax.shard_map(
        make_on_device(mesh),
        mesh=mesh,
        in_specs=placed,
        out_specs=(
            P(tokens, None),
            P(tokens),
            P("fsdp", EXPERT),
            P("fsdp", EXPERT),
            P(EXPERT, "fsdp"),
        ),
        check_vma=False,
    )
```

```python
import jax
import jax.numpy as jnp
from jax import lax
from jax.experimental import pallas as pl
from jax.experimental.pallas import tpu as pltpu
from jax.sharding import Mesh
from jax.sharding import PartitionSpec as P

CAP = 8
PLANE = ("x", "y")
EXPERT = ("x", "y", "core")
CORE_FIRST = ("core", "x", "y")
LANES = 128
BLOCK = 128
BF16 = jnp.bfloat16
F32 = jnp.float32


def contract(left, right, left_dim, right_dim):
    return lax.dot_general(
        left, right, (((left_dim,), (right_dim,)), ((), ())), preferred_element_type=F32
    )


def kernel_call(body, outs, limit, scalars=0, grid=(1,), **specs):
    grid_spec = pltpu.PrefetchScalarGridSpec(num_scalar_prefetch=scalars, grid=grid, **specs)
    return pl.pallas_call(
        body,
        out_shape=outs,
        grid_spec=grid_spec,
        compiler_params=pltpu.CompilerParams(vmem_limit_bytes=limit << 20),
    )


def far_memory():
    return pl.BlockSpec(memory_space=pl.ANY)


def whole(shape):
    return pl.BlockSpec(shape, lambda *_: (0,) * len(shape), pipeline_mode=pl.Buffered(1))


def block_at(shape, where):
    return pl.BlockSpec(shape, lambda *_: where, pipeline_mode=pl.Buffered(1))


def two_lanes(column):
    high = column.astype(BF16).astype(F32)
    lane = lax.broadcasted_iota(jnp.int32, (column.shape[0], LANES), 1)
    spread = jnp.where(lane == 0, high, jnp.where(lane == 1, column - high, 0.0))
    return spread.astype(BF16)


def scaled_weights(gate_quant, gate_scale, up_quant, up_scale, down_quant, down_scale):
    part, units = gate_quant.shape
    half = part // 2

    def body(gate, up, down, gate_s, up_s, down_s, first, second):
        for i in range(part // BLOCK):
            rows = slice(i * BLOCK, (i + 1) * BLOCK)
            out, at = (first, i * BLOCK) if i * BLOCK < half else (second, i * BLOCK - half)
            for j in range(units // BLOCK):
                cols = slice(j * BLOCK, (j + 1) * BLOCK)
                tiles = (
                    gate[rows, cols].astype(F32) * gate_s[i, j],
                    up[rows, cols].astype(F32) * up_s[i, j],
                    (down[cols, rows].astype(F32) * down_s[j, i]).T,
                )
                for k, tile in enumerate(tiles):
                    to = k * units + j * BLOCK
                    out[at : at + BLOCK, to : to + BLOCK] = tile.astype(BF16)

    quants, scales = [gate_quant, up_quant, down_quant], [gate_scale, up_scale, down_scale]
    shape = (half, 3 * units)
    return kernel_call(
        body,
        (jax.ShapeDtypeStruct(shape, BF16),) * 2,
        16,
        in_specs=[whole(v.shape) for v in quants] + [pl.BlockSpec(memory_space=pltpu.SMEM)] * 3,
        out_specs=(whole(shape),) * 2,
    )(*quants, *scales)


def pre_sums(rows, first_parts, second_parts):
    count = len(first_parts)
    half, wide = first_parts[0][1].shape
    part, both = 2 * half, wide // 3 * 2
    slots = rows.shape[0]
    width = (rows.shape[1] - LANES) // 2
    places = [r for r, _ in first_parts]
    assert places == [r for r, _ in second_parts]

    def body(rows_ref, *refs):
        weights, out = refs[: 2 * count], refs[2 * count]
        x_in, dy_in, weights_in, sems = refs[2 * count + 1 :]
        copies = []
        for i, r in enumerate(places):
            pairs = (
                (rows_ref.at[:, pl.ds(r * part, part)], x_in.at[i]),
                (rows_ref.at[:, pl.ds(width + r * part, part)], dy_in.at[i]),
                (weights[i], weights_in.at[i, pl.ds(0, half)]),
                (weights[count + i], weights_in.at[i, pl.ds(half, half)]),
            )
            copies.append(
                [
                    pltpu.make_async_copy(source, into, sems.at[k, i])
                    for k, (source, into) in enumerate(pairs)
                ]
            )
            for copy in copies[-1]:
                copy.start()
        pre = back = None
        for i in range(count):
            for copy in copies[i]:
                copy.wait()
            one = contract(x_in[i], weights_in[i, :, :both], 1, 0)
            two = contract(dy_in[i], weights_in[i, :, both:], 1, 0)
            pre = one if pre is None else pre + one
            back = two if back is None else back + two
        out[:, :both] = pre
        out[:, both:] = back

    weights = [w for _, w in first_parts] + [w for _, w in second_parts]
    shape = (slots, wide)
    return kernel_call(
        body,
        jax.ShapeDtypeStruct(shape, F32),
        60,
        in_specs=[far_memory()] * (1 + 2 * count),
        out_specs=whole(shape),
        scratch_shapes=[
            pltpu.VMEM((count, slots, part), BF16),
            pltpu.VMEM((count, slots, part), BF16),
            pltpu.VMEM((count, part, wide), BF16),
            pltpu.SemaphoreType.DMA((4, count)),
        ],
    )(rows, *weights)


def activations(rows, sums, first_part, second_part):
    count = rows.shape[0]
    far, first = first_part
    second = second_part[1]
    half, wide = first.shape
    part, units = 2 * half, wide // 3
    both = 2 * units
    width = (rows.shape[1] - LANES) // 2

    def body(x_ref, dy_ref, prob_ref, sums_ref, first_ref, second_ref, acts_ref, prob_out):
        pre = sums_ref[:, :both] + contract(x_ref[:, :half], first_ref[:, :both], 1, 0)
        pre = pre + contract(x_ref[:, half:], second_ref[:, :both], 1, 0)
        back = sums_ref[:, both:] + contract(dy_ref[:, :half], first_ref[:, both:], 1, 0)
        back = back + contract(dy_ref[:, half:], second_ref[:, both:], 1, 0)
        gate_pre, up_pre = pre[:, :units], pre[:, units:]
        sigmoid_gate = jax.nn.sigmoid(gate_pre)
        hidden = (gate_pre * sigmoid_gate * up_pre).astype(BF16)
        prob_part = jnp.sum(hidden.astype(F32) * back, axis=1, keepdims=True)
        grad_hidden = prob_ref[:, :1].astype(F32) * back
        acts_ref[:, :units] = (
            grad_hidden * up_pre * sigmoid_gate * (1.0 + gate_pre * (1.0 - sigmoid_gate))
        ).astype(BF16)
        acts_ref[:, units:both] = (grad_hidden * gate_pre * sigmoid_gate).astype(BF16)
        acts_ref[:, both:] = hidden
        prob_out[...] = two_lanes(prob_part)

    acts_shape, prob_shape = (count, both + units), (count, LANES)
    return kernel_call(
        body,
        (jax.ShapeDtypeStruct(acts_shape, BF16), jax.ShapeDtypeStruct(prob_shape, BF16)),
        60,
        in_specs=[
            block_at((count, part), (0, far)),
            block_at((count, part), (0, width // part + far)),
            block_at((count, LANES), (0, 2 * width // LANES)),
            whole(sums.shape),
            whole(first.shape),
            whole(second.shape),
        ],
        out_specs=(whole(acts_shape), whole(prob_shape)),
    )(rows, rows, rows, sums, first, second)


def slot_sums(core, acts, prob_lanes, first_parts, second_parts):
    rows_half = acts.shape[0] // 2
    count = len(first_parts)
    half, wide = first_parts[0][1].shape
    part, both = 2 * half, wide // 3 * 2
    width = count * part
    places = [r for r, _ in first_parts]
    assert places == [r for r, _ in second_parts]

    def body(core_ref, acts_ref, prob_ref, *refs):
        weights, give, keep, weights_in, sems = refs[: 2 * count], *refs[2 * count :]
        copies = []
        for i in range(count):
            for k in range(2):
                copy = pltpu.make_async_copy(
                    weights[k * count + i].at[:, pl.ds(0, both)],
                    weights_in.at[i, pl.ds(k * half, half)],
                    sems.at[k, i],
                )
                copy.start()
                copies.append(copy)
        theirs = pl.ds(pl.multiple_of((1 - core_ref[0]) * rows_half, rows_half), rows_half)
        mine = pl.ds(pl.multiple_of(core_ref[0] * rows_half, rows_half), rows_half)
        acts = jnp.concatenate([acts_ref[theirs, :both], acts_ref[mine, :both]], axis=0)
        for i, r in enumerate(places):
            copies[2 * i].wait()
            copies[2 * i + 1].wait()
            sums = contract(acts, weights_in[i], 1, 1).astype(BF16)
            give[:, r * part : (r + 1) * part] = sums[:rows_half]
            keep[:, r * part : (r + 1) * part] = sums[rows_half:]
        give[:, width:] = prob_ref[theirs, :]
        keep[:, width:] = prob_ref[mine, :]

    weights = [w for _, w in first_parts] + [w for _, w in second_parts]
    shape = (rows_half, width + LANES)
    return kernel_call(
        body,
        (jax.ShapeDtypeStruct(shape, BF16),) * 2,
        60,
        scalars=1,
        in_specs=[whole(acts.shape), whole(prob_lanes.shape)] + [far_memory()] * (2 * count),
        out_specs=(whole(shape),) * 2,
        scratch_shapes=[
            pltpu.VMEM((count, part, both), BF16),
            pltpu.SemaphoreType.DMA((2, count)),
        ],
    )(core, acts, prob_lanes, *weights)


def pair_sum(mine, other):
    width = mine.shape[1] - LANES

    def body(a_ref, b_ref, out):
        for at in range(0, width, 768):
            cols = slice(at, at + 768)
            out[:, cols] = (a_ref[:, cols].astype(F32) + b_ref[:, cols].astype(F32)).astype(BF16)
        lanes = a_ref[:, width:].astype(F32) + b_ref[:, width:].astype(F32)
        out[:, width:] = two_lanes(lanes[:, 0:1] + lanes[:, 1:2])

    return kernel_call(
        body,
        jax.ShapeDtypeStruct(mine.shape, BF16),
        16,
        in_specs=[whole(mine.shape)] * 2,
        out_specs=whole(mine.shape),
    )(mine, other)


def weight_sums(columns, acts):
    slots, twice = columns.shape
    part, units = twice // 2, acts.shape[1] // 3
    tile = 256
    steps = part // tile

    def body(x_ref, weighted_ref, acts_ref, gate_out, up_out, down_out):
        both = contract(x_ref[...], acts_ref[:, : 2 * units], 0, 0)
        gate_out[...] = both[:, :units]
        up_out[...] = both[:, units:]
        down_out[...] = contract(acts_ref[:, 2 * units :], weighted_ref[...], 0, 0)

    return kernel_call(
        body,
        (
            jax.ShapeDtypeStruct((part, units), F32),
            jax.ShapeDtypeStruct((part, units), F32),
            jax.ShapeDtypeStruct((units, part), F32),
        ),
        60,
        grid=(steps,),
        in_specs=[
            pl.BlockSpec((slots, tile), lambda i: (0, i)),
            pl.BlockSpec((slots, tile), lambda i: (0, steps + i)),
            whole(acts.shape),
        ],
        out_specs=(
            pl.BlockSpec((tile, units), lambda i: (i, 0)),
            pl.BlockSpec((tile, units), lambda i: (i, 0)),
            pl.BlockSpec((units, tile), lambda i: (0, i)),
        ),
    )(columns, columns, acts)


def turn(values, axis, place, size):
    flipped = jnp.flip(values, axis)
    twice = jnp.concatenate([flipped, flipped], axis)
    return lax.dynamic_slice_in_dim(twice, size - 1 - place, size, axis)


def ring_gather(block, axis, size, last_up):
    up = [(i, (i + 1) % size) for i in range(size)]
    down = [(i, (i - 1) % size) for i in range(size)]
    far = size // 2
    parts = [(0, block)]
    ahead, behind = block, block
    for step in range(1, far):
        ahead = lax.ppermute(ahead, axis, up)
        behind = lax.ppermute(behind, axis, down)
        parts += [(step, ahead), (size - step, behind)]
    last = lax.ppermute(ahead, axis, up) if last_up else lax.ppermute(behind, axis, down)
    return parts, (far, last)


def make_on_device(mesh):
    ring = mesh.shape["fsdp"]

    def on_device(
        x_quant,
        x_scale,
        grad_out,
        route_mask,
        route_prob,
        gate_quant,
        gate_scale,
        up_quant,
        up_scale,
        down_quant,
        down_scale,
    ):
        place = lax.axis_index("fsdp")
        core = lax.axis_index("core")
        width = x_quant.shape[1]
        part = width // ring

        first, second = scaled_weights(
            gate_quant, gate_scale, up_quant, up_scale, down_quant, down_scale
        )
        first_near, first_far = ring_gather(first, "fsdp", ring, True)
        second_near, second_far = ring_gather(second, "fsdp", ring, False)

        slot_rank = jnp.cumsum(route_mask) - 1
        slot_ids = jnp.arange(CAP, dtype=jnp.int32)
        table = ((slot_rank[None, :] == slot_ids[:, None]) & (route_mask[None, :] == 1)).astype(BF16)
        table_wide = table.astype(F32)
        blocks = x_scale.shape[1]
        slot_quant = jnp.dot(table, x_quant, preferred_element_type=F32)
        slot_scale = jnp.dot(
            table_wide, x_scale, precision=lax.Precision.HIGHEST, preferred_element_type=F32
        )
        slot_x = (
            (slot_quant.reshape(CAP, blocks, width // blocks) * slot_scale[:, :, None])
            .reshape(CAP, width)
            .astype(BF16)
        )
        slot_dy = jnp.dot(table, grad_out, preferred_element_type=F32).astype(BF16)
        slot_prob = jnp.sum(table_wide * route_prob.astype(F32)[None, :], axis=1)
        weighted = (slot_prob[:, None] * slot_dy.astype(F32)).astype(BF16)

        sides = jnp.concatenate(
            [slot_x.reshape(CAP, ring, part), weighted.reshape(CAP, ring, part)], axis=-1
        ).transpose(1, 0, 2)
        turned = turn(
            jnp.stack([slot_x, slot_dy]).reshape(2, CAP, ring, part), 2, place, ring
        ).reshape(2, CAP, width)
        packed = jnp.concatenate(
            [turned[0], turned[1], jnp.broadcast_to(slot_prob.astype(BF16)[:, None], (CAP, 128))],
            axis=1,
        )
        rows = lax.all_gather(packed, CORE_FIRST, axis=0, tiled=True)

        sides = lax.all_to_all(sides, "fsdp", split_axis=0, concat_axis=0, tiled=True)
        sides, *_ = lax.optimization_barrier(
            (sides, *(w for _, w in first_near[1:3] + second_near[1:3]))
        )
        columns = lax.all_gather(sides, CORE_FIRST, axis=1, tiled=True).reshape(-1, 2 * part)

        sums = pre_sums(rows, first_near, second_near)
        acts, prob_lanes = activations(rows, sums, first_far, second_far)
        all_acts = lax.all_gather(acts, "fsdp", axis=0, tiled=True)

        give, keep = slot_sums(
            core[None], acts, prob_lanes, [*first_near, first_far], [*second_near, second_far]
        )
        got = lax.ppermute(give, "core", [(0, 1), (1, 0)])
        both = pair_sum(keep, got).reshape(-1, CAP, width + LANES)
        shares = lax.all_to_all(both, PLANE, split_axis=0, concat_axis=0, tiled=True)
        mine = jnp.sum(shares.astype(F32), axis=0)
        mine_grad = mine[:, :width].astype(BF16).reshape(CAP, ring, part)
        mine_grad = turn(mine_grad, 1, place, ring).reshape(CAP, width)
        mine_prob = mine[:, width] + mine[:, width + 1]
        grad_x = contract(table, mine_grad, 0, 0).astype(BF16)
        grad_prob = jnp.sum(table_wide * mine_prob[:, None], axis=0)

        grad_gate, grad_up, grad_down = weight_sums(columns, all_acts)
        return (grad_x, grad_prob, grad_gate, grad_up, grad_down)

    return on_device


def solution(mesh):
    devices = mesh.devices
    mesh = Mesh(devices.reshape(devices.shape[0], 4, 4, 2), ("fsdp", "x", "y", "core"))
    tokens = ("fsdp", "x", "y", "core")
    placed = (
        P(tokens, None),
        P(tokens, None),
        P(tokens, None),
        P(tokens),
        P(tokens),
        P("fsdp", EXPERT),
        P("fsdp", EXPERT),
        P("fsdp", EXPERT),
        P("fsdp", EXPERT),
        P(EXPERT, "fsdp"),
        P(EXPERT, "fsdp"),
    )
    return jax.shard_map(
        make_on_device(mesh),
        mesh=mesh,
        in_specs=placed,
        out_specs=(
            P(tokens, None),
            P(tokens),
            P("fsdp", EXPERT),
            P("fsdp", EXPERT),
            P(EXPERT, "fsdp"),
        ),
        check_vma=False,
    )
```

```python
import jax
import jax.numpy as jnp
from jax import lax
from jax.experimental import pallas as pl
from jax.experimental.pallas import tpu as pltpu
from jax.sharding import Mesh
from jax.sharding import PartitionSpec as P

CAP = 8
PLANE = ("x", "y")
EXPERT = ("x", "y", "core")
CORE_FIRST = ("core", "x", "y")
LANES = 128
BLOCK = 128
BF16 = jnp.bfloat16
F32 = jnp.float32


def contract(left, right, left_dim, right_dim):
    return lax.dot_general(
        left, right, (((left_dim,), (right_dim,)), ((), ())), preferred_element_type=F32
    )


def kernel_call(body, outs, limit, scalars=0, grid=(1,), **specs):
    grid_spec = pltpu.PrefetchScalarGridSpec(num_scalar_prefetch=scalars, grid=grid, **specs)
    return pl.pallas_call(
        body,
        out_shape=outs,
        grid_spec=grid_spec,
        compiler_params=pltpu.CompilerParams(vmem_limit_bytes=limit << 20),
    )


def far_memory():
    return pl.BlockSpec(memory_space=pl.ANY)


def whole(shape):
    return pl.BlockSpec(shape, lambda *_: (0,) * len(shape), pipeline_mode=pl.Buffered(1))


def block_at(shape, where):
    return pl.BlockSpec(shape, lambda *_: where, pipeline_mode=pl.Buffered(1))


def two_lanes(column):
    high = column.astype(BF16).astype(F32)
    lane = lax.broadcasted_iota(jnp.int32, (column.shape[0], LANES), 1)
    spread = jnp.where(lane == 0, high, jnp.where(lane == 1, column - high, 0.0))
    return spread.astype(BF16)


def scaled_weights(gate_quant, gate_scale, up_quant, up_scale, down_quant, down_scale):
    part, units = gate_quant.shape
    half = part // 2

    def body(gate, up, down, gate_s, up_s, down_s, first, second):
        for i in range(part // BLOCK):
            rows = slice(i * BLOCK, (i + 1) * BLOCK)
            out, at = (first, i * BLOCK) if i * BLOCK < half else (second, i * BLOCK - half)
            for j in range(units // BLOCK):
                cols = slice(j * BLOCK, (j + 1) * BLOCK)
                tiles = (
                    gate[rows, cols].astype(F32) * gate_s[i, j],
                    up[rows, cols].astype(F32) * up_s[i, j],
                    (down[cols, rows].astype(F32) * down_s[j, i]).T,
                )
                for k, tile in enumerate(tiles):
                    to = k * units + j * BLOCK
                    out[at : at + BLOCK, to : to + BLOCK] = tile.astype(BF16)

    quants, scales = [gate_quant, up_quant, down_quant], [gate_scale, up_scale, down_scale]
    shape = (half, 3 * units)
    return kernel_call(
        body,
        (jax.ShapeDtypeStruct(shape, BF16),) * 2,
        16,
        in_specs=[whole(v.shape) for v in quants] + [pl.BlockSpec(memory_space=pltpu.SMEM)] * 3,
        out_specs=(whole(shape),) * 2,
    )(*quants, *scales)


def pre_sums(rows, first_parts, second_parts):
    count = len(first_parts)
    half, wide = first_parts[0][1].shape
    part, both = 2 * half, wide // 3 * 2
    slots = rows.shape[0]
    width = (rows.shape[1] - LANES) // 2
    places = [r for r, _ in first_parts]
    assert places == [r for r, _ in second_parts]

    def body(rows_ref, *refs):
        weights, out = refs[: 2 * count], refs[2 * count]
        x_in, dy_in, weights_in, sems = refs[2 * count + 1 :]
        copies = []
        for i, r in enumerate(places):
            pairs = (
                (rows_ref.at[:, pl.ds(r * part, part)], x_in.at[i]),
                (rows_ref.at[:, pl.ds(width + r * part, part)], dy_in.at[i]),
                (weights[i], weights_in.at[i, pl.ds(0, half)]),
                (weights[count + i], weights_in.at[i, pl.ds(half, half)]),
            )
            copies.append(
                [
                    pltpu.make_async_copy(source, into, sems.at[k, i])
                    for k, (source, into) in enumerate(pairs)
                ]
            )
            for copy in copies[-1]:
                copy.start()
        pre = back = None
        for i in range(count):
            for copy in copies[i]:
                copy.wait()
            one = contract(x_in[i], weights_in[i, :, :both], 1, 0)
            two = contract(dy_in[i], weights_in[i, :, both:], 1, 0)
            pre = one if pre is None else pre + one
            back = two if back is None else back + two
        out[:, :both] = pre
        out[:, both:] = back

    weights = [w for _, w in first_parts] + [w for _, w in second_parts]
    shape = (slots, wide)
    return kernel_call(
        body,
        jax.ShapeDtypeStruct(shape, F32),
        60,
        in_specs=[far_memory()] * (1 + 2 * count),
        out_specs=whole(shape),
        scratch_shapes=[
            pltpu.VMEM((count, slots, part), BF16),
            pltpu.VMEM((count, slots, part), BF16),
            pltpu.VMEM((count, part, wide), BF16),
            pltpu.SemaphoreType.DMA((4, count)),
        ],
    )(rows, *weights)


def activations(rows, sums, first_part, second_part):
    count = rows.shape[0]
    far, first = first_part
    second = second_part[1]
    half, wide = first.shape
    part, units = 2 * half, wide // 3
    both = 2 * units
    width = (rows.shape[1] - LANES) // 2

    def body(x_ref, dy_ref, prob_ref, sums_ref, first_ref, second_ref, acts_ref, prob_out):
        pre = sums_ref[:, :both] + contract(x_ref[:, :half], first_ref[:, :both], 1, 0)
        pre = pre + contract(x_ref[:, half:], second_ref[:, :both], 1, 0)
        back = sums_ref[:, both:] + contract(dy_ref[:, :half], first_ref[:, both:], 1, 0)
        back = back + contract(dy_ref[:, half:], second_ref[:, both:], 1, 0)
        gate_pre, up_pre = pre[:, :units], pre[:, units:]
        sigmoid_gate = jax.nn.sigmoid(gate_pre)
        hidden = (gate_pre * sigmoid_gate * up_pre).astype(BF16)
        prob_part = jnp.sum(hidden.astype(F32) * back, axis=1, keepdims=True)
        grad_hidden = prob_ref[:, :1].astype(F32) * back
        acts_ref[:, :units] = (
            grad_hidden * up_pre * sigmoid_gate * (1.0 + gate_pre * (1.0 - sigmoid_gate))
        ).astype(BF16)
        acts_ref[:, units:both] = (grad_hidden * gate_pre * sigmoid_gate).astype(BF16)
        acts_ref[:, both:] = hidden
        prob_out[...] = two_lanes(prob_part)

    acts_shape, prob_shape = (count, both + units), (count, LANES)
    return kernel_call(
        body,
        (jax.ShapeDtypeStruct(acts_shape, BF16), jax.ShapeDtypeStruct(prob_shape, BF16)),
        60,
        in_specs=[
            block_at((count, part), (0, far)),
            block_at((count, part), (0, width // part + far)),
            block_at((count, LANES), (0, 2 * width // LANES)),
            whole(sums.shape),
            whole(first.shape),
            whole(second.shape),
        ],
        out_specs=(whole(acts_shape), whole(prob_shape)),
    )(rows, rows, rows, sums, first, second)


def slot_sums(core, acts, prob_lanes, first_parts, second_parts):
    rows_half = acts.shape[0] // 2
    count = len(first_parts)
    half, wide = first_parts[0][1].shape
    part, both = 2 * half, wide // 3 * 2
    width = count * part
    places = [r for r, _ in first_parts]
    assert places == [r for r, _ in second_parts]

    def body(core_ref, acts_ref, prob_ref, *refs):
        weights, give, keep, weights_in, sems = refs[: 2 * count], *refs[2 * count :]
        copies = []
        for i in range(count):
            for k in range(2):
                copy = pltpu.make_async_copy(
                    weights[k * count + i].at[:, pl.ds(0, both)],
                    weights_in.at[i, pl.ds(k * half, half)],
                    sems.at[k, i],
                )
                copy.start()
                copies.append(copy)
        theirs = pl.ds(pl.multiple_of((1 - core_ref[0]) * rows_half, rows_half), rows_half)
        mine = pl.ds(pl.multiple_of(core_ref[0] * rows_half, rows_half), rows_half)
        acts = jnp.concatenate([acts_ref[theirs, :both], acts_ref[mine, :both]], axis=0)
        for i, r in enumerate(places):
            copies[2 * i].wait()
            copies[2 * i + 1].wait()
            sums = contract(acts, weights_in[i], 1, 1).astype(BF16)
            give[:, r * part : (r + 1) * part] = sums[:rows_half]
            keep[:, r * part : (r + 1) * part] = sums[rows_half:]
        give[:, width:] = prob_ref[theirs, :]
        keep[:, width:] = prob_ref[mine, :]

    weights = [w for _, w in first_parts] + [w for _, w in second_parts]
    shape = (rows_half, width + LANES)
    return kernel_call(
        body,
        (jax.ShapeDtypeStruct(shape, BF16),) * 2,
        60,
        scalars=1,
        in_specs=[whole(acts.shape), whole(prob_lanes.shape)] + [far_memory()] * (2 * count),
        out_specs=(whole(shape),) * 2,
        scratch_shapes=[
            pltpu.VMEM((count, part, both), BF16),
            pltpu.SemaphoreType.DMA((2, count)),
        ],
    )(core, acts, prob_lanes, *weights)


def pair_sum(mine, other):
    width = mine.shape[1] - LANES

    def body(a_ref, b_ref, out):
        for at in range(0, width, 768):
            cols = slice(at, at + 768)
            out[:, cols] = (a_ref[:, cols].astype(F32) + b_ref[:, cols].astype(F32)).astype(BF16)
        lanes = a_ref[:, width:].astype(F32) + b_ref[:, width:].astype(F32)
        out[:, width:] = two_lanes(lanes[:, 0:1] + lanes[:, 1:2])

    return kernel_call(
        body,
        jax.ShapeDtypeStruct(mine.shape, BF16),
        16,
        in_specs=[whole(mine.shape)] * 2,
        out_specs=whole(mine.shape),
    )(mine, other)


def turned_features(columns, part):
    slots = columns.shape[0]
    tile = 256

    def body(x_ref, out):
        out[...] = x_ref[...].astype(F32).T.astype(BF16)

    return kernel_call(
        body,
        jax.ShapeDtypeStruct((part, slots), BF16),
        16,
        grid=(slots // tile,),
        in_specs=[pl.BlockSpec((tile, part), lambda i: (i, 0))],
        out_specs=pl.BlockSpec((part, tile), lambda i: (0, i)),
    )(columns)


def weight_sums(features, columns, acts):
    part, slots = features.shape
    units = acts.shape[1] // 3
    tile = 256
    steps = part // tile

    def body(x_ref, weighted_ref, acts_ref, gate_out, up_out, down_out, hidden):
        @pl.when(pl.program_id(0) == 0)
        def _():
            for at in range(0, slots, tile):
                hidden[:, at : at + tile] = (
                    acts_ref[at : at + tile, 2 * units :].astype(F32).T.astype(BF16)
                )

        both = contract(x_ref[...], acts_ref[:, : 2 * units], 1, 0)
        gate_out[...] = both[:, :units]
        up_out[...] = both[:, units:]
        down_out[...] = contract(hidden[...], weighted_ref[...], 1, 0)

    return kernel_call(
        body,
        (
            jax.ShapeDtypeStruct((part, units), F32),
            jax.ShapeDtypeStruct((part, units), F32),
            jax.ShapeDtypeStruct((units, part), F32),
        ),
        60,
        grid=(steps,),
        in_specs=[
            pl.BlockSpec((tile, slots), lambda i: (i, 0)),
            pl.BlockSpec((slots, tile), lambda i: (0, steps + i)),
            whole(acts.shape),
        ],
        out_specs=(
            pl.BlockSpec((tile, units), lambda i: (i, 0)),
            pl.BlockSpec((tile, units), lambda i: (i, 0)),
            pl.BlockSpec((units, tile), lambda i: (0, i)),
        ),
        scratch_shapes=[pltpu.VMEM((units, slots), BF16)],
    )(features, columns, acts)


def pick_slots(place, mask, prob, x_quant, x_scale, grad_out, ring):
    tokens, width = x_quant.shape
    part = width // ring

    def body(place_ref, mask_ref, prob_ref, x_ref, scale_ref, dy_ref, rows, sides, slot_out):
        mask = mask_ref[...]
        earlier = lax.broadcasted_iota(jnp.int32, (tokens, tokens), 0)
        later = lax.broadcasted_iota(jnp.int32, (tokens, tokens), 1)
        upto = (earlier <= later).astype(F32).astype(BF16)
        ones = jnp.broadcast_to(mask, (CAP, tokens)).astype(F32)
        rank = contract(ones.astype(BF16), upto, 1, 0) - 1.0
        wanted = lax.broadcasted_iota(jnp.int32, (CAP, tokens), 0).astype(F32)
        table = jnp.where((rank == wanted) & (ones == 1.0), 1.0, 0.0)
        slot_out[...] = jnp.where(mask == 1, rank[:1].astype(jnp.int32), -1)
        picked = table.astype(BF16)
        scale = lax.dot_general(
            table,
            scale_ref[...],
            (((1,), (0,)), ((), ())),
            precision=lax.Precision.HIGHEST,
            preferred_element_type=F32,
        )
        slot_prob = jnp.sum(table * prob_ref[...].astype(F32), axis=1, keepdims=True)
        for d in range(ring):
            cols = slice(d * part, (d + 1) * part)
            turned = ((place_ref[0] - d) & (ring - 1)) * part
            quant = contract(picked, x_ref[:, cols], 1, 0)
            x = jnp.concatenate(
                [
                    quant[:, k * BLOCK : (k + 1) * BLOCK]
                    * scale[:, d * part // BLOCK + k : d * part // BLOCK + k + 1]
                    for k in range(part // BLOCK)
                ],
                axis=1,
            ).astype(BF16)
            dy = contract(picked, dy_ref[:, cols], 1, 0)
            rows[:, pl.ds(pl.multiple_of(turned, BLOCK), part)] = x
            rows[:, pl.ds(pl.multiple_of(width + turned, BLOCK), part)] = dy.astype(BF16)
            sides[d, :, :part] = x
            sides[d, :, part:] = (slot_prob * dy).astype(BF16)
        rows[:, 2 * width :] = jnp.broadcast_to(slot_prob, (CAP, LANES)).astype(BF16)

    shapes = ((CAP, 2 * width + LANES), (ring, CAP, 2 * part), (1, tokens))
    inputs = [mask.reshape(1, tokens), prob.reshape(1, tokens), x_quant, x_scale, grad_out]
    return kernel_call(
        body,
        tuple(
            jax.ShapeDtypeStruct(v, t) for v, t in zip(shapes, (BF16, BF16, jnp.int32))
        ),
        24,
        scalars=1,
        in_specs=[whole(v.shape) for v in inputs],
        out_specs=tuple(whole(v) for v in shapes),
    )(place[None], *inputs)


def turn(values, axis, place, size):
    flipped = jnp.flip(values, axis)
    twice = jnp.concatenate([flipped, flipped], axis)
    return lax.dynamic_slice_in_dim(twice, size - 1 - place, size, axis)


def ring_gather(block, axis, size, last_up):
    up = [(i, (i + 1) % size) for i in range(size)]
    down = [(i, (i - 1) % size) for i in range(size)]
    far = size // 2
    parts = [(0, block)]
    ahead, behind = block, block
    for step in range(1, far):
        ahead = lax.ppermute(ahead, axis, up)
        behind = lax.ppermute(behind, axis, down)
        parts += [(step, ahead), (size - step, behind)]
    last = lax.ppermute(ahead, axis, up) if last_up else lax.ppermute(behind, axis, down)
    return parts, (far, last)


def make_on_device(mesh):
    ring = mesh.shape["fsdp"]

    def on_device(
        x_quant,
        x_scale,
        grad_out,
        route_mask,
        route_prob,
        gate_quant,
        gate_scale,
        up_quant,
        up_scale,
        down_quant,
        down_scale,
    ):
        place = lax.axis_index("fsdp")
        core = lax.axis_index("core")
        width = x_quant.shape[1]
        part = width // ring

        first, second = scaled_weights(
            gate_quant, gate_scale, up_quant, up_scale, down_quant, down_scale
        )
        first_near, first_far = ring_gather(first, "fsdp", ring, True)
        second_near, second_far = ring_gather(second, "fsdp", ring, False)

        packed, sides, token_slot = pick_slots(
            place, route_mask, route_prob, x_quant, x_scale, grad_out, ring
        )
        rows = lax.all_gather(packed, CORE_FIRST, axis=0, tiled=True)

        sides = lax.all_to_all(sides, "fsdp", split_axis=0, concat_axis=0, tiled=True)
        sides, *_ = lax.optimization_barrier(
            (sides, *(w for _, w in first_near[1:3] + second_near[1:3]))
        )
        columns = lax.all_gather(sides, CORE_FIRST, axis=1, tiled=True).reshape(-1, 2 * part)

        sums = pre_sums(rows, first_near, second_near)
        acts, prob_lanes = activations(rows, sums, first_far, second_far)
        all_acts = lax.all_gather(acts, "fsdp", axis=0, tiled=True)

        give, keep = slot_sums(
            core[None], acts, prob_lanes, [*first_near, first_far], [*second_near, second_far]
        )
        got = lax.ppermute(give, "core", [(0, 1), (1, 0)])
        both = pair_sum(keep, got).reshape(-1, CAP, width + LANES)
        shares = lax.all_to_all(both, PLANE, split_axis=0, concat_axis=0, tiled=True)
        table = token_slot == jnp.arange(CAP, dtype=jnp.int32)[:, None]
        mine = jnp.sum(shares.astype(F32), axis=0)
        mine_grad = mine[:, :width].astype(BF16).reshape(CAP, ring, part)
        mine_grad = turn(mine_grad, 1, place, ring).reshape(CAP, width)
        mine_prob = mine[:, width] + mine[:, width + 1]
        grad_x = contract(table.astype(BF16), mine_grad, 0, 0).astype(BF16)
        grad_prob = jnp.sum(jnp.where(table, mine_prob[:, None], 0.0), axis=0)

        grad_gate, grad_up, grad_down = weight_sums(
            turned_features(columns, part), columns, all_acts
        )
        return (grad_x, grad_prob, grad_gate, grad_up, grad_down)

    return on_device


def solution(mesh):
    devices = mesh.devices
    mesh = Mesh(devices.reshape(devices.shape[0], 4, 4, 2), ("fsdp", "x", "y", "core"))
    tokens = ("fsdp", "x", "y", "core")
    placed = (
        P(tokens, None),
        P(tokens, None),
        P(tokens, None),
        P(tokens),
        P(tokens),
        P("fsdp", EXPERT),
        P("fsdp", EXPERT),
        P("fsdp", EXPERT),
        P("fsdp", EXPERT),
        P(EXPERT, "fsdp"),
        P(EXPERT, "fsdp"),
    )
    return jax.shard_map(
        make_on_device(mesh),
        mesh=mesh,
        in_specs=placed,
        out_specs=(
            P(tokens, None),
            P(tokens),
            P("fsdp", EXPERT),
            P("fsdp", EXPERT),
            P(EXPERT, "fsdp"),
        ),
        check_vma=False,
    )
```

```python
import jax
import jax.numpy as jnp
from jax import lax
from jax.experimental import pallas as pl
from jax.experimental.pallas import tpu as pltpu
from jax.sharding import Mesh
from jax.sharding import PartitionSpec as P

CAP = 8
PLANE = ("x", "y")
EXPERT = ("x", "y", "core")
CORE_FIRST = ("core", "x", "y")
LANES = 128
BLOCK = 128
BF16 = jnp.bfloat16
F32 = jnp.float32


def contract(left, right, left_dim, right_dim):
    return lax.dot_general(
        left, right, (((left_dim,), (right_dim,)), ((), ())), preferred_element_type=F32
    )


def kernel_call(body, outs, limit, scalars=0, grid=(1,), **specs):
    grid_spec = pltpu.PrefetchScalarGridSpec(num_scalar_prefetch=scalars, grid=grid, **specs)
    return pl.pallas_call(
        body,
        out_shape=outs,
        grid_spec=grid_spec,
        compiler_params=pltpu.CompilerParams(vmem_limit_bytes=limit << 20),
    )


def far_memory():
    return pl.BlockSpec(memory_space=pl.ANY)


def whole(shape):
    return pl.BlockSpec(shape, lambda *_: (0,) * len(shape), pipeline_mode=pl.Buffered(1))


def block_at(shape, where):
    return pl.BlockSpec(shape, lambda *_: where, pipeline_mode=pl.Buffered(1))


def two_lanes(column):
    high = column.astype(BF16).astype(F32)
    lane = lax.broadcasted_iota(jnp.int32, (column.shape[0], LANES), 1)
    spread = jnp.where(lane == 0, high, jnp.where(lane == 1, column - high, 0.0))
    return spread.astype(BF16)


def scaled_weights(gate_quant, gate_scale, up_quant, up_scale, down_quant, down_scale):
    part, units = gate_quant.shape
    half = part // 2

    def body(gate, up, down, gate_s, up_s, down_s, first, second):
        for i in range(part // BLOCK):
            rows = slice(i * BLOCK, (i + 1) * BLOCK)
            out, at = (first, i * BLOCK) if i * BLOCK < half else (second, i * BLOCK - half)
            for j in range(units // BLOCK):
                cols = slice(j * BLOCK, (j + 1) * BLOCK)
                tiles = (
                    gate[rows, cols].astype(F32) * gate_s[j, i],
                    up[rows, cols].astype(F32) * up_s[j, i],
                    (down[cols, rows].astype(F32) * down_s[j, i]).T,
                )
                for k, tile in enumerate(tiles):
                    to = k * units + j * BLOCK
                    out[at : at + BLOCK, to : to + BLOCK] = tile.astype(BF16)

    quants, scales = [gate_quant, up_quant, down_quant], [gate_scale.T, up_scale.T, down_scale]
    shape = (half, 3 * units)
    return kernel_call(
        body,
        (jax.ShapeDtypeStruct(shape, BF16),) * 2,
        60,
        in_specs=[whole(v.shape) for v in quants] + [pl.BlockSpec(memory_space=pltpu.SMEM)] * 3,
        out_specs=(whole(shape),) * 2,
    )(*quants, *scales)


def pre_sums(rows, first_parts, second_parts):
    count = len(first_parts)
    half, wide = first_parts[0][1].shape
    part, both = 2 * half, wide // 3 * 2
    slots = rows.shape[0]
    width = (rows.shape[1] - LANES) // 2
    places = [r for r, _ in first_parts]
    assert places == [r for r, _ in second_parts]

    def body(rows_ref, *refs):
        weights, out = refs[: 2 * count], refs[2 * count]
        x_in, dy_in, weights_in, sems = refs[2 * count + 1 :]
        copies = []
        for i, r in enumerate(places):
            pairs = (
                (rows_ref.at[:, pl.ds(r * part, part)], x_in.at[i]),
                (rows_ref.at[:, pl.ds(width + r * part, part)], dy_in.at[i]),
                (weights[i], weights_in.at[i, pl.ds(0, half)]),
                (weights[count + i], weights_in.at[i, pl.ds(half, half)]),
            )
            copies.append(
                [
                    pltpu.make_async_copy(source, into, sems.at[k, i])
                    for k, (source, into) in enumerate(pairs)
                ]
            )
            for copy in copies[-1]:
                copy.start()
        pre = back = None
        for i in range(count):
            for copy in copies[i]:
                copy.wait()
            one = contract(x_in[i], weights_in[i, :, :both], 1, 0)
            two = contract(dy_in[i], weights_in[i, :, both:], 1, 0)
            pre = one if pre is None else pre + one
            back = two if back is None else back + two
        out[:, :both] = pre
        out[:, both:] = back

    weights = [w for _, w in first_parts] + [w for _, w in second_parts]
    shape = (slots, wide)
    return kernel_call(
        body,
        jax.ShapeDtypeStruct(shape, F32),
        60,
        in_specs=[far_memory()] * (1 + 2 * count),
        out_specs=whole(shape),
        scratch_shapes=[
            pltpu.VMEM((count, slots, part), BF16),
            pltpu.VMEM((count, slots, part), BF16),
            pltpu.VMEM((count, part, wide), BF16),
            pltpu.SemaphoreType.DMA((4, count)),
        ],
    )(rows, *weights)


def activations(rows, sums, first_part, second_part):
    count = rows.shape[0]
    far, first = first_part
    second = second_part[1]
    half, wide = first.shape
    part, units = 2 * half, wide // 3
    both = 2 * units
    width = (rows.shape[1] - LANES) // 2

    def body(x_ref, dy_ref, prob_ref, sums_ref, first_ref, second_ref, acts_ref, prob_out):
        pre = sums_ref[:, :both] + contract(x_ref[:, :half], first_ref[:, :both], 1, 0)
        pre = pre + contract(x_ref[:, half:], second_ref[:, :both], 1, 0)
        back = sums_ref[:, both:] + contract(dy_ref[:, :half], first_ref[:, both:], 1, 0)
        back = back + contract(dy_ref[:, half:], second_ref[:, both:], 1, 0)
        gate_pre, up_pre = pre[:, :units], pre[:, units:]
        sigmoid_gate = jax.nn.sigmoid(gate_pre)
        hidden = (gate_pre * sigmoid_gate * up_pre).astype(BF16)
        prob_part = jnp.sum(hidden.astype(F32) * back, axis=1, keepdims=True)
        grad_hidden = prob_ref[:, :1].astype(F32) * back
        acts_ref[:, :units] = (
            grad_hidden * up_pre * sigmoid_gate * (1.0 + gate_pre * (1.0 - sigmoid_gate))
        ).astype(BF16)
        acts_ref[:, units:both] = (grad_hidden * gate_pre * sigmoid_gate).astype(BF16)
        acts_ref[:, both:] = hidden
        prob_out[...] = two_lanes(prob_part)

    acts_shape, prob_shape = (count, both + units), (count, LANES)
    return kernel_call(
        body,
        (jax.ShapeDtypeStruct(acts_shape, BF16), jax.ShapeDtypeStruct(prob_shape, BF16)),
        60,
        in_specs=[
            block_at((count, part), (0, far)),
            block_at((count, part), (0, width // part + far)),
            block_at((count, LANES), (0, 2 * width // LANES)),
            whole(sums.shape),
            whole(first.shape),
            whole(second.shape),
        ],
        out_specs=(whole(acts_shape), whole(prob_shape)),
    )(rows, rows, rows, sums, first, second)


def slot_sums(core, acts, prob_lanes, first_parts, second_parts):
    rows_half = acts.shape[0] // 2
    count = len(first_parts)
    half, wide = first_parts[0][1].shape
    part, both = 2 * half, wide // 3 * 2
    width = count * part
    places = [r for r, _ in first_parts]
    assert places == [r for r, _ in second_parts]

    def body(core_ref, acts_ref, prob_ref, *refs):
        weights, give, keep, weights_in, sems = refs[: 2 * count], *refs[2 * count :]
        copies = []
        for i in range(count):
            for k in range(2):
                copy = pltpu.make_async_copy(
                    weights[k * count + i].at[:, pl.ds(0, both)],
                    weights_in.at[i, pl.ds(k * half, half)],
                    sems.at[k, i],
                )
                copy.start()
                copies.append(copy)
        theirs = pl.ds(pl.multiple_of((1 - core_ref[0]) * rows_half, rows_half), rows_half)
        mine = pl.ds(pl.multiple_of(core_ref[0] * rows_half, rows_half), rows_half)
        acts = jnp.concatenate([acts_ref[theirs, :both], acts_ref[mine, :both]], axis=0)
        for i, r in enumerate(places):
            copies[2 * i].wait()
            copies[2 * i + 1].wait()
            sums = contract(acts, weights_in[i], 1, 1).astype(BF16)
            give[:, r * part : (r + 1) * part] = sums[:rows_half]
            keep[:, r * part : (r + 1) * part] = sums[rows_half:]
        give[:, width:] = prob_ref[theirs, :]
        keep[:, width:] = prob_ref[mine, :]

    weights = [w for _, w in first_parts] + [w for _, w in second_parts]
    shape = (rows_half, width + LANES)
    return kernel_call(
        body,
        (jax.ShapeDtypeStruct(shape, BF16),) * 2,
        60,
        scalars=1,
        in_specs=[whole(acts.shape), whole(prob_lanes.shape)] + [far_memory()] * (2 * count),
        out_specs=(whole(shape),) * 2,
        scratch_shapes=[
            pltpu.VMEM((count, part, both), BF16),
            pltpu.SemaphoreType.DMA((2, count)),
        ],
    )(core, acts, prob_lanes, *weights)


def pair_sum(mine, other):
    width = mine.shape[1] - LANES

    def body(a_ref, b_ref, out):
        for at in range(0, width, 768):
            cols = slice(at, at + 768)
            out[:, cols] = (a_ref[:, cols].astype(F32) + b_ref[:, cols].astype(F32)).astype(BF16)
        lanes = a_ref[:, width:].astype(F32) + b_ref[:, width:].astype(F32)
        out[:, width:] = two_lanes(lanes[:, 0:1] + lanes[:, 1:2])

    return kernel_call(
        body,
        jax.ShapeDtypeStruct(mine.shape, BF16),
        16,
        in_specs=[whole(mine.shape)] * 2,
        out_specs=whole(mine.shape),
    )(mine, other)


def split_columns(columns, part):
    slots = columns.shape[0]
    tile = 256

    def body(x_ref, weighted_ref, features, weighted):
        features[...] = x_ref[...].astype(F32).T.astype(BF16)
        weighted[...] = weighted_ref[...]

    return kernel_call(
        body,
        (
            jax.ShapeDtypeStruct((part, slots), BF16),
            jax.ShapeDtypeStruct((slots, part), BF16),
        ),
        16,
        grid=(slots // tile,),
        in_specs=[
            pl.BlockSpec((tile, part), lambda i: (i, 0)),
            pl.BlockSpec((tile, part), lambda i: (i, 1)),
        ],
        out_specs=(
            pl.BlockSpec((part, tile), lambda i: (0, i)),
            pl.BlockSpec((tile, part), lambda i: (i, 0)),
        ),
    )(columns, columns)


def weight_sums(features, weighted, acts):
    part, slots = features.shape
    units = acts.shape[1] // 3

    def body(x_ref, weighted_ref, acts_ref, gate_out, up_out, down_out):
        gate_up = contract(x_ref[...], acts_ref[:, : 2 * units], 1, 0)
        gate_out[...] = gate_up[:, :units]
        up_out[...] = gate_up[:, units:]
        down_out[...] = contract(acts_ref[:, 2 * units :], weighted_ref[...], 0, 0)

    shapes = ((part, units), (part, units), (units, part))
    return kernel_call(
        body,
        tuple(jax.ShapeDtypeStruct(v, F32) for v in shapes),
        55,
        in_specs=[whole(features.shape), whole(weighted.shape), whole(acts.shape)],
        out_specs=tuple(whole(v) for v in shapes),
    )(features, weighted, acts)


def pick_slots(place, mask, prob, x_quant, x_scale, grad_out, ring):
    tokens, width = x_quant.shape
    part = width // ring

    def body(place_ref, mask_ref, prob_ref, x_ref, scale_ref, dy_ref, rows, sides, slot_out):
        mask = mask_ref[...]
        earlier = lax.broadcasted_iota(jnp.int32, (tokens, tokens), 0)
        later = lax.broadcasted_iota(jnp.int32, (tokens, tokens), 1)
        upto = (earlier <= later).astype(F32).astype(BF16)
        ones = jnp.broadcast_to(mask, (CAP, tokens)).astype(F32)
        rank = contract(ones.astype(BF16), upto, 1, 0) - 1.0
        wanted = lax.broadcasted_iota(jnp.int32, (CAP, tokens), 0).astype(F32)
        table = jnp.where((rank == wanted) & (ones == 1.0), 1.0, 0.0)
        slot_out[...] = jnp.where(mask == 1, rank[:1].astype(jnp.int32), -1)
        picked = table.astype(BF16)
        scale = lax.dot_general(
            table,
            scale_ref[...],
            (((1,), (1,)), ((), ())),
            precision=lax.Precision.HIGHEST,
            preferred_element_type=F32,
        )
        slot_prob = jnp.sum(table * prob_ref[...].astype(F32), axis=1, keepdims=True)
        for d in range(ring):
            cols = slice(d * part, (d + 1) * part)
            turned = ((place_ref[0] - d) & (ring - 1)) * part
            quant = contract(picked, x_ref[:, cols], 1, 0)
            x = jnp.concatenate(
                [
                    quant[:, k * BLOCK : (k + 1) * BLOCK]
                    * scale[:, d * part // BLOCK + k : d * part // BLOCK + k + 1]
                    for k in range(part // BLOCK)
                ],
                axis=1,
            ).astype(BF16)
            dy = contract(picked, dy_ref[:, cols], 1, 0)
            rows[:, pl.ds(pl.multiple_of(turned, BLOCK), part)] = x
            rows[:, pl.ds(pl.multiple_of(width + turned, BLOCK), part)] = dy.astype(BF16)
            sides[d, :, :part] = x
            sides[d, :, part:] = (slot_prob * dy).astype(BF16)
        rows[:, 2 * width :] = jnp.broadcast_to(slot_prob, (CAP, LANES)).astype(BF16)

    shapes = ((CAP, 2 * width + LANES), (ring, CAP, 2 * part), (1, tokens))
    inputs = [mask.reshape(1, tokens), prob.reshape(1, tokens), x_quant, x_scale.T, grad_out]
    return kernel_call(
        body,
        tuple(
            jax.ShapeDtypeStruct(v, t) for v, t in zip(shapes, (BF16, BF16, jnp.int32))
        ),
        60,
        scalars=1,
        in_specs=[whole(v.shape) for v in inputs],
        out_specs=tuple(whole(v) for v in shapes),
    )(place[None], *inputs)


def turn(values, axis, place, size):
    flipped = jnp.flip(values, axis)
    twice = jnp.concatenate([flipped, flipped], axis)
    return lax.dynamic_slice_in_dim(twice, size - 1 - place, size, axis)


def ring_gather(block, axis, size, last_up):
    up = [(i, (i + 1) % size) for i in range(size)]
    down = [(i, (i - 1) % size) for i in range(size)]
    far = size // 2
    parts = [(0, block)]
    ahead, behind = block, block
    for step in range(1, far):
        ahead = lax.ppermute(ahead, axis, up)
        behind = lax.ppermute(behind, axis, down)
        parts += [(step, ahead), (size - step, behind)]
    last = lax.ppermute(ahead, axis, up) if last_up else lax.ppermute(behind, axis, down)
    return parts, (far, last)


def make_on_device(mesh):
    ring = mesh.shape["fsdp"]

    def on_device(
        x_quant,
        x_scale,
        grad_out,
        route_mask,
        route_prob,
        gate_quant,
        gate_scale,
        up_quant,
        up_scale,
        down_quant,
        down_scale,
    ):
        place = lax.axis_index("fsdp")
        core = lax.axis_index("core")
        width = x_quant.shape[1]
        part = width // ring

        first, second = scaled_weights(
            gate_quant, gate_scale, up_quant, up_scale, down_quant, down_scale
        )
        first_near, first_far = ring_gather(first, "fsdp", ring, True)
        second_near, second_far = ring_gather(second, "fsdp", ring, False)

        packed, sides, token_slot = pick_slots(
            place, route_mask, route_prob, x_quant, x_scale, grad_out, ring
        )
        rows = lax.all_gather(packed, CORE_FIRST, axis=0, tiled=True)

        sides = lax.all_to_all(sides, "fsdp", split_axis=0, concat_axis=0, tiled=True)
        sides, *_ = lax.optimization_barrier(
            (sides, *(w for _, w in first_near[1:3] + second_near[1:3]))
        )
        columns = lax.all_gather(sides, CORE_FIRST, axis=1, tiled=True).reshape(-1, 2 * part)

        sums = pre_sums(rows, first_near, second_near)
        acts, prob_lanes = activations(rows, sums, first_far, second_far)
        all_acts = lax.all_gather(acts, "fsdp", axis=0, tiled=True)

        give, keep = slot_sums(
            core[None], acts, prob_lanes, [*first_near, first_far], [*second_near, second_far]
        )
        got = lax.ppermute(give, "core", [(0, 1), (1, 0)])
        both = pair_sum(keep, got).reshape(-1, CAP, width + LANES)
        shares = lax.all_to_all(both, PLANE, split_axis=0, concat_axis=0, tiled=True)
        table = token_slot == jnp.arange(CAP, dtype=jnp.int32)[:, None]
        mine = jnp.sum(shares.astype(F32), axis=0)
        mine_grad = mine[:, :width].astype(BF16).reshape(CAP, ring, part)
        mine_grad = turn(mine_grad, 1, place, ring).reshape(CAP, width)
        mine_prob = mine[:, width] + mine[:, width + 1]
        grad_x = contract(table.astype(BF16), mine_grad, 0, 0).astype(BF16)
        grad_prob = jnp.sum(jnp.where(table, mine_prob[:, None], 0.0), axis=0)

        grad_gate, grad_up, grad_down = weight_sums(
            *split_columns(columns, part), all_acts
        )
        return (grad_x, grad_prob, grad_gate, grad_up, grad_down)

    return on_device


def solution(mesh):
    devices = mesh.devices
    mesh = Mesh(devices.reshape(devices.shape[0], 4, 4, 2), ("fsdp", "x", "y", "core"))
    tokens = ("fsdp", "x", "y", "core")
    placed = (
        P(tokens, None),
        P(tokens, None),
        P(tokens, None),
        P(tokens),
        P(tokens),
        P("fsdp", EXPERT),
        P("fsdp", EXPERT),
        P("fsdp", EXPERT),
        P("fsdp", EXPERT),
        P(EXPERT, "fsdp"),
        P(EXPERT, "fsdp"),
    )
    return jax.shard_map(
        make_on_device(mesh),
        mesh=mesh,
        in_specs=placed,
        out_specs=(
            P(tokens, None),
            P(tokens),
            P("fsdp", EXPERT),
            P("fsdp", EXPERT),
            P(EXPERT, "fsdp"),
        ),
        check_vma=False,
    )
```

```python
import jax
import jax.numpy as jnp
from jax import lax
from jax.experimental import pallas as pl
from jax.experimental.pallas import tpu as pltpu
from jax.sharding import Mesh
from jax.sharding import PartitionSpec as P

CAP = 8
PLANE = ("x", "y")
EXPERT = ("x", "y", "core")
CORE_FIRST = ("core", "x", "y")
LANES = 128
BLOCK = 128
BF16 = jnp.bfloat16
F32 = jnp.float32


def contract(left, right, left_dim, right_dim):
    return lax.dot_general(
        left, right, (((left_dim,), (right_dim,)), ((), ())), preferred_element_type=F32
    )


def kernel_call(body, outs, limit, scalars=0, grid=(1,), **specs):
    grid_spec = pltpu.PrefetchScalarGridSpec(num_scalar_prefetch=scalars, grid=grid, **specs)
    return pl.pallas_call(
        body,
        out_shape=outs,
        grid_spec=grid_spec,
        compiler_params=pltpu.CompilerParams(vmem_limit_bytes=limit << 20),
    )


def far_memory():
    return pl.BlockSpec(memory_space=pl.ANY)


def whole(shape):
    return pl.BlockSpec(shape, lambda *_: (0,) * len(shape), pipeline_mode=pl.Buffered(1))


def block_at(shape, where):
    return pl.BlockSpec(shape, lambda *_: where, pipeline_mode=pl.Buffered(1))


def two_lanes(column):
    high = column.astype(BF16).astype(F32)
    lane = lax.broadcasted_iota(jnp.int32, (column.shape[0], LANES), 1)
    spread = jnp.where(lane == 0, high, jnp.where(lane == 1, column - high, 0.0))
    return spread.astype(BF16)


def scaled_weights(gate_quant, gate_scale, up_quant, up_scale, down_quant, down_scale):
    part, units = gate_quant.shape
    half = part // 2

    def body(gate, up, down, gate_s, up_s, down_s, first, second):
        for i in range(part // BLOCK):
            rows = slice(i * BLOCK, (i + 1) * BLOCK)
            out, at = (first, i * BLOCK) if i * BLOCK < half else (second, i * BLOCK - half)
            for j in range(units // BLOCK):
                cols = slice(j * BLOCK, (j + 1) * BLOCK)
                tiles = (
                    gate[rows, cols].astype(F32) * gate_s[j, i],
                    up[rows, cols].astype(F32) * up_s[j, i],
                    (down[cols, rows].astype(F32) * down_s[j, i]).T,
                )
                for k, tile in enumerate(tiles):
                    to = k * units + j * BLOCK
                    out[at : at + BLOCK, to : to + BLOCK] = tile.astype(BF16)

    quants, scales = [gate_quant, up_quant, down_quant], [gate_scale.T, up_scale.T, down_scale]
    shape = (half, 3 * units)
    return kernel_call(
        body,
        (jax.ShapeDtypeStruct(shape, BF16),) * 2,
        60,
        in_specs=[whole(v.shape) for v in quants] + [pl.BlockSpec(memory_space=pltpu.SMEM)] * 3,
        out_specs=(whole(shape),) * 2,
    )(*quants, *scales)


def pre_sums(rows, width, first_parts, second_parts):
    count = len(first_parts)
    half, wide = first_parts[0][1].shape
    part, both = 2 * half, wide // 3 * 2
    slots = rows.shape[0]
    places = [r for r, _ in first_parts]
    assert places == [r for r, _ in second_parts]

    def body(rows_ref, *refs):
        weights, out = refs[: 2 * count], refs[2 * count]
        x_in, dy_in, weights_in, sems = refs[2 * count + 1 :]
        copies = []
        for i, r in enumerate(places):
            pairs = (
                (rows_ref.at[:, pl.ds(r * part, part)], x_in.at[i]),
                (rows_ref.at[:, pl.ds(width + r * part, part)], dy_in.at[i]),
                (weights[i], weights_in.at[i, pl.ds(0, half)]),
                (weights[count + i], weights_in.at[i, pl.ds(half, half)]),
            )
            copies.append(
                [
                    pltpu.make_async_copy(source, into, sems.at[k, i])
                    for k, (source, into) in enumerate(pairs)
                ]
            )
            for copy in copies[-1]:
                copy.start()
        pre = back = None
        for i in range(count):
            for copy in copies[i]:
                copy.wait()
            one = contract(x_in[i], weights_in[i, :, :both], 1, 0)
            two = contract(dy_in[i], weights_in[i, :, both:], 1, 0)
            pre = one if pre is None else pre + one
            back = two if back is None else back + two
        out[:, :both] = pre
        out[:, both:] = back

    weights = [w for _, w in first_parts] + [w for _, w in second_parts]
    shape = (slots, wide)
    return kernel_call(
        body,
        jax.ShapeDtypeStruct(shape, F32),
        60,
        in_specs=[far_memory()] * (1 + 2 * count),
        out_specs=whole(shape),
        scratch_shapes=[
            pltpu.VMEM((count, slots, part), BF16),
            pltpu.VMEM((count, slots, part), BF16),
            pltpu.VMEM((count, part, wide), BF16),
            pltpu.SemaphoreType.DMA((4, count)),
        ],
    )(rows, *weights)


def activations(rows, width, sums, first_part, second_part):
    count = rows.shape[0]
    far, first = first_part
    second = second_part[1]
    half, wide = first.shape
    part, units = 2 * half, wide // 3
    both = 2 * units

    def body(x_ref, dy_ref, prob_ref, sums_ref, first_ref, second_ref, acts_ref, prob_out):
        pre = sums_ref[:, :both] + contract(x_ref[:, :half], first_ref[:, :both], 1, 0)
        pre = pre + contract(x_ref[:, half:], second_ref[:, :both], 1, 0)
        back = sums_ref[:, both:] + contract(dy_ref[:, :half], first_ref[:, both:], 1, 0)
        back = back + contract(dy_ref[:, half:], second_ref[:, both:], 1, 0)
        gate_pre, up_pre = pre[:, :units], pre[:, units:]
        sigmoid_gate = jax.nn.sigmoid(gate_pre)
        hidden = (gate_pre * sigmoid_gate * up_pre).astype(BF16)
        prob_part = jnp.sum(hidden.astype(F32) * back, axis=1, keepdims=True)
        grad_hidden = prob_ref[:, :1].astype(F32) * back
        acts_ref[:, :units] = (
            grad_hidden * up_pre * sigmoid_gate * (1.0 + gate_pre * (1.0 - sigmoid_gate))
        ).astype(BF16)
        acts_ref[:, units:both] = (grad_hidden * gate_pre * sigmoid_gate).astype(BF16)
        acts_ref[:, both:] = hidden
        prob_out[...] = two_lanes(prob_part)

    acts_shape, prob_shape = (count, both + units), (count, LANES)
    return kernel_call(
        body,
        (jax.ShapeDtypeStruct(acts_shape, BF16), jax.ShapeDtypeStruct(prob_shape, BF16)),
        60,
        in_specs=[
            block_at((count, part), (0, far)),
            block_at((count, part), (0, width // part + far)),
            block_at((count, LANES), (0, 2 * width // LANES)),
            whole(sums.shape),
            whole(first.shape),
            whole(second.shape),
        ],
        out_specs=(whole(acts_shape), whole(prob_shape)),
    )(rows, rows, rows, sums, first, second)


def slot_sums(core, acts, prob_lanes, first_parts, second_parts):
    rows_half = acts.shape[0] // 2
    count = len(first_parts)
    half, wide = first_parts[0][1].shape
    part, both = 2 * half, wide // 3 * 2
    width = count * part
    places = [r for r, _ in first_parts]
    assert places == [r for r, _ in second_parts]

    def body(core_ref, acts_ref, prob_ref, *refs):
        weights, give, keep, weights_in, sems = refs[: 2 * count], *refs[2 * count :]
        copies = []
        for i in range(count):
            for k in range(2):
                copy = pltpu.make_async_copy(
                    weights[k * count + i].at[:, pl.ds(0, both)],
                    weights_in.at[i, pl.ds(k * half, half)],
                    sems.at[k, i],
                )
                copy.start()
                copies.append(copy)
        theirs = pl.ds(pl.multiple_of((1 - core_ref[0]) * rows_half, rows_half), rows_half)
        mine = pl.ds(pl.multiple_of(core_ref[0] * rows_half, rows_half), rows_half)
        acts = jnp.concatenate([acts_ref[theirs, :both], acts_ref[mine, :both]], axis=0)
        for i, r in enumerate(places):
            copies[2 * i].wait()
            copies[2 * i + 1].wait()
            sums = contract(acts, weights_in[i], 1, 1).astype(BF16)
            give[:, r * part : (r + 1) * part] = sums[:rows_half]
            keep[:, r * part : (r + 1) * part] = sums[rows_half:]
        give[:, width:] = prob_ref[theirs, :]
        keep[:, width:] = prob_ref[mine, :]

    weights = [w for _, w in first_parts] + [w for _, w in second_parts]
    shape = (rows_half, width + LANES)
    return kernel_call(
        body,
        (jax.ShapeDtypeStruct(shape, BF16),) * 2,
        60,
        scalars=1,
        in_specs=[whole(acts.shape), whole(prob_lanes.shape)] + [far_memory()] * (2 * count),
        out_specs=(whole(shape),) * 2,
        scratch_shapes=[
            pltpu.VMEM((count, part, both), BF16),
            pltpu.SemaphoreType.DMA((2, count)),
        ],
    )(core, acts, prob_lanes, *weights)


def pair_sum(mine, other):
    width = mine.shape[1] - LANES

    def body(a_ref, b_ref, out):
        for at in range(0, width, 768):
            cols = slice(at, at + 768)
            out[:, cols] = (a_ref[:, cols].astype(F32) + b_ref[:, cols].astype(F32)).astype(BF16)
        lanes = a_ref[:, width:].astype(F32) + b_ref[:, width:].astype(F32)
        out[:, width:] = two_lanes(lanes[:, 0:1] + lanes[:, 1:2])

    return kernel_call(
        body,
        jax.ShapeDtypeStruct(mine.shape, BF16),
        16,
        in_specs=[whole(mine.shape)] * 2,
        out_specs=whole(mine.shape),
    )(mine, other)


def joined(packed, sides):
    ring, _, wide = sides.shape
    start = packed.shape[1]

    def body(packed_ref, sides_ref, out):
        out[:, :start] = packed_ref[...]
        for d in range(ring):
            out[:, start + d * wide : start + (d + 1) * wide] = sides_ref[d]

    shape = (CAP, start + ring * wide)
    return kernel_call(
        body,
        jax.ShapeDtypeStruct(shape, BF16),
        60,
        in_specs=[whole(packed.shape), whole(sides.shape)],
        out_specs=whole(shape),
    )(packed, sides)


def split_columns(rows, start, part, ring):
    slots = rows.shape[0]

    def body(rows_ref, features, weighted, sides, sems):
        copies = [
            pltpu.make_async_copy(
                rows_ref.at[:, pl.ds(start + d * 2 * part, 2 * part)], sides.at[d], sems.at[d]
            )
            for d in range(ring)
        ]
        for copy in copies:
            copy.start()
        for d in range(ring):
            copies[d].wait()
            at = slice(d * slots, (d + 1) * slots)
            features[:, at] = sides[d, :, :part].astype(F32).T.astype(BF16)
            weighted[at, :] = sides[d, :, part:]

    shapes = ((part, ring * slots), (ring * slots, part))
    return kernel_call(
        body,
        tuple(jax.ShapeDtypeStruct(v, BF16) for v in shapes),
        60,
        in_specs=[far_memory()],
        out_specs=tuple(whole(v) for v in shapes),
        scratch_shapes=[
            pltpu.VMEM((ring, slots, 2 * part), BF16),
            pltpu.SemaphoreType.DMA((ring,)),
        ],
    )(rows)


def weight_sums(features, weighted, acts):
    part, slots = features.shape
    units = acts.shape[1] // 3

    def body(x_ref, weighted_ref, acts_ref, gate_out, up_out, down_out):
        gate_up = contract(x_ref[...], acts_ref[:, : 2 * units], 1, 0)
        gate_out[...] = gate_up[:, :units]
        up_out[...] = gate_up[:, units:]
        down_out[...] = contract(acts_ref[:, 2 * units :], weighted_ref[...], 0, 0)

    shapes = ((part, units), (part, units), (units, part))
    return kernel_call(
        body,
        tuple(jax.ShapeDtypeStruct(v, F32) for v in shapes),
        55,
        in_specs=[whole(features.shape), whole(weighted.shape), whole(acts.shape)],
        out_specs=tuple(whole(v) for v in shapes),
    )(features, weighted, acts)


def pick_slots(place, mask, prob, x_quant, x_scale, grad_out, ring):
    tokens, width = x_quant.shape
    part = width // ring

    def body(place_ref, mask_ref, prob_ref, x_ref, scale_ref, dy_ref, rows, sides, slot_out):
        mask = mask_ref[...]
        earlier = lax.broadcasted_iota(jnp.int32, (tokens, tokens), 0)
        later = lax.broadcasted_iota(jnp.int32, (tokens, tokens), 1)
        upto = (earlier <= later).astype(F32).astype(BF16)
        ones = jnp.broadcast_to(mask, (CAP, tokens)).astype(F32)
        rank = contract(ones.astype(BF16), upto, 1, 0) - 1.0
        wanted = lax.broadcasted_iota(jnp.int32, (CAP, tokens), 0).astype(F32)
        table = jnp.where((rank == wanted) & (ones == 1.0), 1.0, 0.0)
        slot_out[...] = jnp.where(mask == 1, rank[:1].astype(jnp.int32), -1)
        picked = table.astype(BF16)
        scale = lax.dot_general(
            table,
            scale_ref[...],
            (((1,), (1,)), ((), ())),
            precision=lax.Precision.HIGHEST,
            preferred_element_type=F32,
        )
        slot_prob = jnp.sum(table * prob_ref[...].astype(F32), axis=1, keepdims=True)
        for d in range(ring):
            cols = slice(d * part, (d + 1) * part)
            turned = ((place_ref[0] - d) & (ring - 1)) * part
            quant = contract(picked, x_ref[:, cols], 1, 0)
            x = jnp.concatenate(
                [
                    quant[:, k * BLOCK : (k + 1) * BLOCK]
                    * scale[:, d * part // BLOCK + k : d * part // BLOCK + k + 1]
                    for k in range(part // BLOCK)
                ],
                axis=1,
            ).astype(BF16)
            dy = contract(picked, dy_ref[:, cols], 1, 0)
            rows[:, pl.ds(pl.multiple_of(turned, BLOCK), part)] = x
            rows[:, pl.ds(pl.multiple_of(width + turned, BLOCK), part)] = dy.astype(BF16)
            sides[d, :, :part] = x
            sides[d, :, part:] = (slot_prob * dy).astype(BF16)
        rows[:, 2 * width :] = jnp.broadcast_to(slot_prob, (CAP, LANES)).astype(BF16)

    shapes = ((CAP, 2 * width + LANES), (ring, CAP, 2 * part), (1, tokens))
    inputs = [mask.reshape(1, tokens), prob.reshape(1, tokens), x_quant, x_scale.T, grad_out]
    return kernel_call(
        body,
        tuple(
            jax.ShapeDtypeStruct(v, t) for v, t in zip(shapes, (BF16, BF16, jnp.int32))
        ),
        60,
        scalars=1,
        in_specs=[whole(v.shape) for v in inputs],
        out_specs=tuple(whole(v) for v in shapes),
    )(place[None], *inputs)


def turn(values, axis, place, size):
    flipped = jnp.flip(values, axis)
    twice = jnp.concatenate([flipped, flipped], axis)
    return lax.dynamic_slice_in_dim(twice, size - 1 - place, size, axis)


def ring_gather(block, axis, size, last_up):
    up = [(i, (i + 1) % size) for i in range(size)]
    down = [(i, (i - 1) % size) for i in range(size)]
    far = size // 2
    parts = [(0, block)]
    ahead, behind = block, block
    for step in range(1, far):
        ahead = lax.ppermute(ahead, axis, up)
        behind = lax.ppermute(behind, axis, down)
        parts += [(step, ahead), (size - step, behind)]
    last = lax.ppermute(ahead, axis, up) if last_up else lax.ppermute(behind, axis, down)
    return parts, (far, last)


def make_on_device(mesh):
    ring = mesh.shape["fsdp"]

    def on_device(
        x_quant,
        x_scale,
        grad_out,
        route_mask,
        route_prob,
        gate_quant,
        gate_scale,
        up_quant,
        up_scale,
        down_quant,
        down_scale,
    ):
        place = lax.axis_index("fsdp")
        core = lax.axis_index("core")
        width = x_quant.shape[1]
        part = width // ring

        first, second = scaled_weights(
            gate_quant, gate_scale, up_quant, up_scale, down_quant, down_scale
        )
        first_near, first_far = ring_gather(first, "fsdp", ring, True)
        second_near, second_far = ring_gather(second, "fsdp", ring, False)

        packed, sides, token_slot = pick_slots(
            place, route_mask, route_prob, x_quant, x_scale, grad_out, ring
        )
        sides = lax.all_to_all(sides, "fsdp", split_axis=0, concat_axis=0, tiled=True)
        sides, *_ = lax.optimization_barrier((sides, *(w for _, w in first_near[1:3])))
        rows = lax.all_gather(joined(packed, sides), CORE_FIRST, axis=0, tiled=True)

        sums = pre_sums(rows, width, first_near, second_near)
        acts, prob_lanes = activations(rows, width, sums, first_far, second_far)
        all_acts = lax.all_gather(acts, "fsdp", axis=0, tiled=True)

        give, keep = slot_sums(
            core[None], acts, prob_lanes, [*first_near, first_far], [*second_near, second_far]
        )
        got = lax.ppermute(give, "core", [(0, 1), (1, 0)])
        both = pair_sum(keep, got).reshape(-1, CAP, width + LANES)
        shares = lax.all_to_all(both, PLANE, split_axis=0, concat_axis=0, tiled=True)
        table = token_slot == jnp.arange(CAP, dtype=jnp.int32)[:, None]
        mine = jnp.sum(shares.astype(F32), axis=0)
        mine_grad = mine[:, :width].astype(BF16).reshape(CAP, ring, part)
        mine_grad = turn(mine_grad, 1, place, ring).reshape(CAP, width)
        mine_prob = mine[:, width] + mine[:, width + 1]
        grad_x = contract(table.astype(BF16), mine_grad, 0, 0).astype(BF16)
        grad_prob = jnp.sum(jnp.where(table, mine_prob[:, None], 0.0), axis=0)

        grad_gate, grad_up, grad_down = weight_sums(
            *split_columns(rows, 2 * width + LANES, part, ring), all_acts
        )
        return (grad_x, grad_prob, grad_gate, grad_up, grad_down)

    return on_device


def solution(mesh):
    devices = mesh.devices
    mesh = Mesh(devices.reshape(devices.shape[0], 4, 4, 2), ("fsdp", "x", "y", "core"))
    tokens = ("fsdp", "x", "y", "core")
    placed = (
        P(tokens, None),
        P(tokens, None),
        P(tokens, None),
        P(tokens),
        P(tokens),
        P("fsdp", EXPERT),
        P("fsdp", EXPERT),
        P("fsdp", EXPERT),
        P("fsdp", EXPERT),
        P(EXPERT, "fsdp"),
        P(EXPERT, "fsdp"),
    )
    return jax.shard_map(
        make_on_device(mesh),
        mesh=mesh,
        in_specs=placed,
        out_specs=(
            P(tokens, None),
            P(tokens),
            P("fsdp", EXPERT),
            P("fsdp", EXPERT),
            P(EXPERT, "fsdp"),
        ),
        check_vma=False,
    )
```

```python
import jax
import jax.numpy as jnp
from jax import lax
from jax.experimental import pallas as pl
from jax.experimental.pallas import tpu as pltpu
from jax.sharding import Mesh
from jax.sharding import PartitionSpec as P

CAP = 8
PLANE = ("x", "y")
EXPERT = ("x", "y", "core")
CORE_FIRST = ("core", "x", "y")
LANES = 128
BLOCK = 128
BF16 = jnp.bfloat16
F32 = jnp.float32


def contract(left, right, left_dim, right_dim):
    return lax.dot_general(
        left, right, (((left_dim,), (right_dim,)), ((), ())), preferred_element_type=F32
    )


def kernel_call(body, outs, limit, scalars=0, grid=(1,), **specs):
    grid_spec = pltpu.PrefetchScalarGridSpec(num_scalar_prefetch=scalars, grid=grid, **specs)
    return pl.pallas_call(
        body,
        out_shape=outs,
        grid_spec=grid_spec,
        compiler_params=pltpu.CompilerParams(vmem_limit_bytes=limit << 20),
    )


def far_memory():
    return pl.BlockSpec(memory_space=pl.ANY)


def whole(shape):
    return pl.BlockSpec(shape, lambda *_: (0,) * len(shape), pipeline_mode=pl.Buffered(1))


def block_at(shape, where):
    return pl.BlockSpec(shape, lambda *_: where, pipeline_mode=pl.Buffered(1))


def two_lanes(column):
    high = column.astype(BF16).astype(F32)
    lane = lax.broadcasted_iota(jnp.int32, (column.shape[0], LANES), 1)
    spread = jnp.where(lane == 0, high, jnp.where(lane == 1, column - high, 0.0))
    return spread.astype(BF16)


def scaled_weights(gate_quant, gate_scale, up_quant, up_scale, down_quant, down_scale, which):
    part, units = gate_quant.shape
    half = part // 2

    def body(gate, up, down, gate_s, up_s, down_s, out):
        for i in range(half // BLOCK):
            rows = slice(i * BLOCK, (i + 1) * BLOCK)
            at = which * half // BLOCK + i
            for j in range(units // BLOCK):
                cols = slice(j * BLOCK, (j + 1) * BLOCK)
                tiles = (
                    gate[rows, cols].astype(F32) * gate_s[j, at],
                    up[rows, cols].astype(F32) * up_s[j, at],
                    (down[cols, rows].astype(F32) * down_s[j, at]).T,
                )
                for k, tile in enumerate(tiles):
                    to = k * units + j * BLOCK
                    out[rows, to : to + BLOCK] = tile.astype(BF16)

    shape = (half, 3 * units)
    return kernel_call(
        body,
        jax.ShapeDtypeStruct(shape, BF16),
        60,
        in_specs=[
            block_at((half, units), (which, 0)),
            block_at((half, units), (which, 0)),
            block_at((units, half), (0, which)),
        ]
        + [pl.BlockSpec(memory_space=pltpu.SMEM)] * 3,
        out_specs=whole(shape),
    )(gate_quant, up_quant, down_quant, gate_scale.T, up_scale.T, down_scale)


def pre_sums(rows, width, first_parts, second_parts):
    count = len(first_parts)
    half, wide = first_parts[0][1].shape
    part, both = 2 * half, wide // 3 * 2
    slots = rows.shape[0]
    places = [r for r, _ in first_parts]
    assert places == [r for r, _ in second_parts]

    def body(rows_ref, *refs):
        weights, out = refs[: 2 * count], refs[2 * count]
        x_in, dy_in, weights_in, sems = refs[2 * count + 1 :]
        copies = []
        for i, r in enumerate(places):
            pairs = (
                (rows_ref.at[:, pl.ds(r * part, part)], x_in.at[i]),
                (rows_ref.at[:, pl.ds(width + r * part, part)], dy_in.at[i]),
                (weights[i], weights_in.at[i, pl.ds(0, half)]),
                (weights[count + i], weights_in.at[i, pl.ds(half, half)]),
            )
            copies.append(
                [
                    pltpu.make_async_copy(source, into, sems.at[k, i])
                    for k, (source, into) in enumerate(pairs)
                ]
            )
            for copy in copies[-1]:
                copy.start()
        pre = back = None
        for i in range(count):
            for copy in copies[i]:
                copy.wait()
            one = contract(x_in[i], weights_in[i, :, :both], 1, 0)
            two = contract(dy_in[i], weights_in[i, :, both:], 1, 0)
            pre = one if pre is None else pre + one
            back = two if back is None else back + two
        out[:, :both] = pre
        out[:, both:] = back

    weights = [w for _, w in first_parts] + [w for _, w in second_parts]
    shape = (slots, wide)
    return kernel_call(
        body,
        jax.ShapeDtypeStruct(shape, F32),
        60,
        in_specs=[far_memory()] * (1 + 2 * count),
        out_specs=whole(shape),
        scratch_shapes=[
            pltpu.VMEM((count, slots, part), BF16),
            pltpu.VMEM((count, slots, part), BF16),
            pltpu.VMEM((count, part, wide), BF16),
            pltpu.SemaphoreType.DMA((4, count)),
        ],
    )(rows, *weights)


def activations(rows, width, sums, first_part, second_part):
    count = rows.shape[0]
    far, first = first_part
    second = second_part[1]
    half, wide = first.shape
    part, units = 2 * half, wide // 3
    both = 2 * units

    def body(x_ref, dy_ref, prob_ref, sums_ref, first_ref, second_ref, acts_ref, prob_out):
        pre = sums_ref[:, :both] + contract(x_ref[:, :half], first_ref[:, :both], 1, 0)
        pre = pre + contract(x_ref[:, half:], second_ref[:, :both], 1, 0)
        back = sums_ref[:, both:] + contract(dy_ref[:, :half], first_ref[:, both:], 1, 0)
        back = back + contract(dy_ref[:, half:], second_ref[:, both:], 1, 0)
        gate_pre, up_pre = pre[:, :units], pre[:, units:]
        sigmoid_gate = jax.nn.sigmoid(gate_pre)
        hidden = (gate_pre * sigmoid_gate * up_pre).astype(BF16)
        prob_part = jnp.sum(hidden.astype(F32) * back, axis=1, keepdims=True)
        grad_hidden = prob_ref[:, :1].astype(F32) * back
        acts_ref[:, :units] = (
            grad_hidden * up_pre * sigmoid_gate * (1.0 + gate_pre * (1.0 - sigmoid_gate))
        ).astype(BF16)
        acts_ref[:, units:both] = (grad_hidden * gate_pre * sigmoid_gate).astype(BF16)
        acts_ref[:, both:] = hidden
        prob_out[...] = two_lanes(prob_part)

    acts_shape, prob_shape = (count, both + units), (count, LANES)
    return kernel_call(
        body,
        (jax.ShapeDtypeStruct(acts_shape, BF16), jax.ShapeDtypeStruct(prob_shape, BF16)),
        60,
        in_specs=[
            block_at((count, part), (0, far)),
            block_at((count, part), (0, width // part + far)),
            block_at((count, LANES), (0, 2 * width // LANES)),
            whole(sums.shape),
            whole(first.shape),
            whole(second.shape),
        ],
        out_specs=(whole(acts_shape), whole(prob_shape)),
    )(rows, rows, rows, sums, first, second)


def slot_sums(core, acts, prob_lanes, first_parts, second_parts):
    rows_half = acts.shape[0] // 2
    count = len(first_parts)
    half, wide = first_parts[0][1].shape
    part, both = 2 * half, wide // 3 * 2
    width = count * part
    places = [r for r, _ in first_parts]
    assert places == [r for r, _ in second_parts]

    def body(core_ref, acts_ref, prob_ref, *refs):
        weights, give, keep, weights_in, sems = refs[: 2 * count], *refs[2 * count :]
        copies = []
        for i in range(count):
            for k in range(2):
                copy = pltpu.make_async_copy(
                    weights[k * count + i].at[:, pl.ds(0, both)],
                    weights_in.at[i, pl.ds(k * half, half)],
                    sems.at[k, i],
                )
                copy.start()
                copies.append(copy)
        theirs = pl.ds(pl.multiple_of((1 - core_ref[0]) * rows_half, rows_half), rows_half)
        mine = pl.ds(pl.multiple_of(core_ref[0] * rows_half, rows_half), rows_half)
        acts = jnp.concatenate([acts_ref[theirs, :both], acts_ref[mine, :both]], axis=0)
        for i, r in enumerate(places):
            copies[2 * i].wait()
            copies[2 * i + 1].wait()
            sums = contract(acts, weights_in[i], 1, 1).astype(BF16)
            give[:, r * part : (r + 1) * part] = sums[:rows_half]
            keep[:, r * part : (r + 1) * part] = sums[rows_half:]
        give[:, width:] = prob_ref[theirs, :]
        keep[:, width:] = prob_ref[mine, :]

    weights = [w for _, w in first_parts] + [w for _, w in second_parts]
    shape = (rows_half, width + LANES)
    return kernel_call(
        body,
        (jax.ShapeDtypeStruct(shape, BF16),) * 2,
        60,
        scalars=1,
        in_specs=[whole(acts.shape), whole(prob_lanes.shape)] + [far_memory()] * (2 * count),
        out_specs=(whole(shape),) * 2,
        scratch_shapes=[
            pltpu.VMEM((count, part, both), BF16),
            pltpu.SemaphoreType.DMA((2, count)),
        ],
    )(core, acts, prob_lanes, *weights)


def pair_sum(mine, other):
    width = mine.shape[1] - LANES

    def body(a_ref, b_ref, out):
        for at in range(0, width, 768):
            cols = slice(at, at + 768)
            out[:, cols] = (a_ref[:, cols].astype(F32) + b_ref[:, cols].astype(F32)).astype(BF16)
        lanes = a_ref[:, width:].astype(F32) + b_ref[:, width:].astype(F32)
        out[:, width:] = two_lanes(lanes[:, 0:1] + lanes[:, 1:2])

    return kernel_call(
        body,
        jax.ShapeDtypeStruct(mine.shape, BF16),
        16,
        in_specs=[whole(mine.shape)] * 2,
        out_specs=whole(mine.shape),
    )(mine, other)


def joined(packed, sides):
    ring, _, wide = sides.shape
    start = packed.shape[1]

    def body(packed_ref, sides_ref, out):
        out[:, :start] = packed_ref[...]
        for d in range(ring):
            out[:, start + d * wide : start + (d + 1) * wide] = sides_ref[d]

    shape = (CAP, start + ring * wide)
    return kernel_call(
        body,
        jax.ShapeDtypeStruct(shape, BF16),
        60,
        in_specs=[whole(packed.shape), whole(sides.shape)],
        out_specs=whole(shape),
    )(packed, sides)


def turned_columns(rows, start, part, ring):
    slots = rows.shape[0]

    def body(rows_ref, out, sides, sems):
        copies = [
            pltpu.make_async_copy(
                rows_ref.at[:, pl.ds(start + d * 2 * part, 2 * part)], sides.at[d], sems.at[d]
            )
            for d in range(ring)
        ]
        for copy in copies:
            copy.start()
        for d in range(ring):
            copies[d].wait()
            out[:, d * slots : (d + 1) * slots] = sides[d].astype(F32).T.astype(BF16)

    shape = (2 * part, ring * slots)
    return kernel_call(
        body,
        jax.ShapeDtypeStruct(shape, BF16),
        60,
        in_specs=[far_memory()],
        out_specs=whole(shape),
        scratch_shapes=[
            pltpu.VMEM((ring, slots, 2 * part), BF16),
            pltpu.SemaphoreType.DMA((ring,)),
        ],
    )(rows)


def weight_sums(columns, acts):
    twice, slots = columns.shape
    part = twice // 2
    wide = acts.shape[1]
    units = wide // 3
    both = 2 * units
    steps = 4
    span = slots // steps

    def body(columns_ref, acts_ref, gate_out, up_out, down_out, cols_in, acts_in, sums, sems):
        copies = []
        for i in range(steps):
            at = pl.ds(i * span, span)
            copies.append(
                (
                    pltpu.make_async_copy(acts_ref.at[at], acts_in.at[i], sems.at[0, i]),
                    pltpu.make_async_copy(columns_ref.at[:, at], cols_in.at[i], sems.at[1, i]),
                )
            )
            for copy in copies[-1]:
                copy.start()
        for i in range(steps):
            for copy in copies[i]:
                copy.wait()
            one = contract(cols_in[i, :part], acts_in[i, :, :both], 1, 0)
            two = contract(cols_in[i, part:], acts_in[i, :, both:], 1, 0)
            if i > 0:
                one, two = sums[:, :both] + one, sums[:, both:] + two
            if i < steps - 1:
                sums[:, :both] = one
                sums[:, both:] = two
            else:
                gate_out[...] = one[:, :units]
                up_out[...] = one[:, units:]
                down_out[...] = two.T

    shapes = ((part, units), (part, units), (units, part))
    return kernel_call(
        body,
        tuple(jax.ShapeDtypeStruct(v, F32) for v in shapes),
        60,
        in_specs=[far_memory()] * 2,
        out_specs=tuple(whole(v) for v in shapes),
        scratch_shapes=[
            pltpu.VMEM((steps, twice, span), BF16),
            pltpu.VMEM((steps, span, wide), BF16),
            pltpu.VMEM((part, wide), F32),
            pltpu.SemaphoreType.DMA((2, steps)),
        ],
    )(columns, acts)


def pick_slots(place, mask, prob, x_quant, x_scale, grad_out, ring):
    tokens, width = x_quant.shape
    part = width // ring

    def body(place_ref, mask_ref, prob_ref, x_ref, scale_ref, dy_ref, rows, sides, slot_out):
        mask = mask_ref[...]
        earlier = lax.broadcasted_iota(jnp.int32, (tokens, tokens), 0)
        later = lax.broadcasted_iota(jnp.int32, (tokens, tokens), 1)
        upto = (earlier <= later).astype(F32).astype(BF16)
        ones = jnp.broadcast_to(mask, (CAP, tokens)).astype(F32)
        rank = contract(ones.astype(BF16), upto, 1, 0) - 1.0
        wanted = lax.broadcasted_iota(jnp.int32, (CAP, tokens), 0).astype(F32)
        table = jnp.where((rank == wanted) & (ones == 1.0), 1.0, 0.0)
        slot_out[...] = jnp.where(mask == 1, rank[:1].astype(jnp.int32), -1)
        picked = table.astype(BF16)
        scale = lax.dot_general(
            table,
            scale_ref[...],
            (((1,), (1,)), ((), ())),
            precision=lax.Precision.HIGHEST,
            preferred_element_type=F32,
        )
        slot_prob = jnp.sum(table * prob_ref[...].astype(F32), axis=1, keepdims=True)
        for d in range(ring):
            cols = slice(d * part, (d + 1) * part)
            turned = ((place_ref[0] - d) & (ring - 1)) * part
            quant = contract(picked, x_ref[:, cols], 1, 0)
            x = jnp.concatenate(
                [
                    quant[:, k * BLOCK : (k + 1) * BLOCK]
                    * scale[:, d * part // BLOCK + k : d * part // BLOCK + k + 1]
                    for k in range(part // BLOCK)
                ],
                axis=1,
            ).astype(BF16)
            dy = contract(picked, dy_ref[:, cols], 1, 0)
            rows[:, pl.ds(pl.multiple_of(turned, BLOCK), part)] = x
            rows[:, pl.ds(pl.multiple_of(width + turned, BLOCK), part)] = dy.astype(BF16)
            sides[d, :, :part] = x
            sides[d, :, part:] = (slot_prob * dy).astype(BF16)
        rows[:, 2 * width :] = jnp.broadcast_to(slot_prob, (CAP, LANES)).astype(BF16)

    shapes = ((CAP, 2 * width + LANES), (ring, CAP, 2 * part), (1, tokens))
    inputs = [mask.reshape(1, tokens), prob.reshape(1, tokens), x_quant, x_scale.T, grad_out]
    return kernel_call(
        body,
        tuple(
            jax.ShapeDtypeStruct(v, t) for v, t in zip(shapes, (BF16, BF16, jnp.int32))
        ),
        60,
        scalars=1,
        in_specs=[whole(v.shape) for v in inputs],
        out_specs=tuple(whole(v) for v in shapes),
    )(place[None], *inputs)


def turn(values, axis, place, size):
    flipped = jnp.flip(values, axis)
    twice = jnp.concatenate([flipped, flipped], axis)
    return lax.dynamic_slice_in_dim(twice, size - 1 - place, size, axis)


def ring_gather(block, axis, size, last_up):
    up = [(i, (i + 1) % size) for i in range(size)]
    down = [(i, (i - 1) % size) for i in range(size)]
    far = size // 2
    parts = [(0, block)]
    ahead, behind = block, block
    for step in range(1, far):
        ahead = lax.ppermute(ahead, axis, up)
        behind = lax.ppermute(behind, axis, down)
        parts += [(step, ahead), (size - step, behind)]
    last = lax.ppermute(ahead, axis, up) if last_up else lax.ppermute(behind, axis, down)
    return parts, (far, last)


def make_on_device(mesh):
    ring = mesh.shape["fsdp"]

    def on_device(
        x_quant,
        x_scale,
        grad_out,
        route_mask,
        route_prob,
        gate_quant,
        gate_scale,
        up_quant,
        up_scale,
        down_quant,
        down_scale,
    ):
        place = lax.axis_index("fsdp")
        core = lax.axis_index("core")
        width = x_quant.shape[1]
        part = width // ring

        first, second = (
            scaled_weights(
                gate_quant, gate_scale, up_quant, up_scale, down_quant, down_scale, which
            )
            for which in range(2)
        )
        first_near, first_far = ring_gather(first, "fsdp", ring, True)
        second_near, second_far = ring_gather(second, "fsdp", ring, False)

        packed, sides, token_slot = pick_slots(
            place, route_mask, route_prob, x_quant, x_scale, grad_out, ring
        )
        sides = lax.all_to_all(sides, "fsdp", split_axis=0, concat_axis=0, tiled=True)
        sides, *_ = lax.optimization_barrier((sides, *(w for _, w in first_near[1:3])))
        rows = lax.all_gather(joined(packed, sides), CORE_FIRST, axis=0, tiled=True)

        sums = pre_sums(rows, width, first_near, second_near)
        acts, prob_lanes = activations(rows, width, sums, first_far, second_far)
        all_acts = lax.all_gather(acts, "fsdp", axis=0, tiled=True)

        give, keep = slot_sums(
            core[None], acts, prob_lanes, [*first_near, first_far], [*second_near, second_far]
        )
        got = lax.ppermute(give, "core", [(0, 1), (1, 0)])
        both = pair_sum(keep, got).reshape(-1, CAP, width + LANES)
        shares = lax.all_to_all(both, PLANE, split_axis=0, concat_axis=0, tiled=True)
        grad_gate, grad_up, grad_down = weight_sums(
            turned_columns(rows, 2 * width + LANES, part, ring), all_acts
        )
        shares, grad_up = lax.optimization_barrier((shares, grad_up))
        table = token_slot == jnp.arange(CAP, dtype=jnp.int32)[:, None]
        mine = jnp.sum(shares.astype(F32), axis=0)
        mine_grad = mine[:, :width].astype(BF16).reshape(CAP, ring, part)
        mine_grad = turn(mine_grad, 1, place, ring).reshape(CAP, width)
        mine_prob = mine[:, width] + mine[:, width + 1]
        grad_x = contract(table.astype(BF16), mine_grad, 0, 0).astype(BF16)
        grad_prob = jnp.sum(jnp.where(table, mine_prob[:, None], 0.0), axis=0)

        return (grad_x, grad_prob, grad_gate, grad_up, grad_down)

    return on_device


def solution(mesh):
    devices = mesh.devices
    mesh = Mesh(devices.reshape(devices.shape[0], 4, 4, 2), ("fsdp", "x", "y", "core"))
    tokens = ("fsdp", "x", "y", "core")
    placed = (
        P(tokens, None),
        P(tokens, None),
        P(tokens, None),
        P(tokens),
        P(tokens),
        P("fsdp", EXPERT),
        P("fsdp", EXPERT),
        P("fsdp", EXPERT),
        P("fsdp", EXPERT),
        P(EXPERT, "fsdp"),
        P(EXPERT, "fsdp"),
    )
    return jax.shard_map(
        make_on_device(mesh),
        mesh=mesh,
        in_specs=placed,
        out_specs=(
            P(tokens, None),
            P(tokens),
            P("fsdp", EXPERT),
            P("fsdp", EXPERT),
            P(EXPERT, "fsdp"),
        ),
        check_vma=False,
    )
```

```python
import jax
import jax.numpy as jnp
from jax import lax
from jax.experimental import pallas as pl
from jax.experimental.pallas import tpu as pltpu
from jax.sharding import Mesh
from jax.sharding import PartitionSpec as P

CAP = 8
PLANE = ("x", "y")
EXPERT = ("x", "y", "core")
CORE_FIRST = ("core", "x", "y")
LANES = 128
BLOCK = 128
BF16 = jnp.bfloat16
F32 = jnp.float32


def contract(left, right, left_dim, right_dim):
    return lax.dot_general(
        left, right, (((left_dim,), (right_dim,)), ((), ())), preferred_element_type=F32
    )


def kernel_call(body, outs, limit, scalars=0, grid=(1,), **specs):
    grid_spec = pltpu.PrefetchScalarGridSpec(num_scalar_prefetch=scalars, grid=grid, **specs)
    return pl.pallas_call(
        body,
        out_shape=outs,
        grid_spec=grid_spec,
        compiler_params=pltpu.CompilerParams(vmem_limit_bytes=limit << 20),
    )


def far_memory():
    return pl.BlockSpec(memory_space=pl.ANY)


def whole(shape):
    return pl.BlockSpec(shape, lambda *_: (0,) * len(shape), pipeline_mode=pl.Buffered(1))


def block_at(shape, where):
    return pl.BlockSpec(shape, lambda *_: where, pipeline_mode=pl.Buffered(1))


def two_lanes(column):
    high = column.astype(BF16).astype(F32)
    lane = lax.broadcasted_iota(jnp.int32, (column.shape[0], LANES), 1)
    spread = jnp.where(lane == 0, high, jnp.where(lane == 1, column - high, 0.0))
    return spread.astype(BF16)


def scaled_weights(gate_quant, gate_scale, up_quant, up_scale, down_quant, down_scale):
    part, units = gate_quant.shape
    half = part // 2

    def body(gate, up, down, gate_s, up_s, down_s, first, second):
        for i in range(part // BLOCK):
            rows = slice(i * BLOCK, (i + 1) * BLOCK)
            out, at = (first, i * BLOCK) if i * BLOCK < half else (second, i * BLOCK - half)
            for j in range(units // BLOCK):
                cols = slice(j * BLOCK, (j + 1) * BLOCK)
                tiles = (
                    gate[rows, cols].astype(F32) * gate_s[j, i],
                    up[rows, cols].astype(F32) * up_s[j, i],
                    (down[cols, rows].astype(F32) * down_s[j, i]).T,
                )
                for k, tile in enumerate(tiles):
                    to = k * units + j * BLOCK
                    out[at : at + BLOCK, to : to + BLOCK] = tile.astype(BF16)

    quants, scales = [gate_quant, up_quant, down_quant], [gate_scale.T, up_scale.T, down_scale]
    shape = (half, 3 * units)
    return kernel_call(
        body,
        (jax.ShapeDtypeStruct(shape, BF16),) * 2,
        60,
        in_specs=[whole(v.shape) for v in quants] + [pl.BlockSpec(memory_space=pltpu.SMEM)] * 3,
        out_specs=(whole(shape),) * 2,
    )(*quants, *scales)


def pre_sums(rows, width, first_parts, second_parts):
    count = len(first_parts)
    half, wide = first_parts[0][1].shape
    part, both = 2 * half, wide // 3 * 2
    slots = rows.shape[0]
    places = [r for r, _ in first_parts]
    assert places == [r for r, _ in second_parts]

    def body(rows_ref, *refs):
        weights, out = refs[: 2 * count], refs[2 * count]
        x_in, dy_in, weights_in, sems = refs[2 * count + 1 :]
        copies = []
        for i, r in enumerate(places):
            pairs = (
                (rows_ref.at[:, pl.ds(r * part, part)], x_in.at[i]),
                (rows_ref.at[:, pl.ds(width + r * part, part)], dy_in.at[i]),
                (weights[i], weights_in.at[i, pl.ds(0, half)]),
                (weights[count + i], weights_in.at[i, pl.ds(half, half)]),
            )
            copies.append(
                [
                    pltpu.make_async_copy(source, into, sems.at[k, i])
                    for k, (source, into) in enumerate(pairs)
                ]
            )
            for copy in copies[-1]:
                copy.start()
        pre = back = None
        for i in range(count):
            for copy in copies[i]:
                copy.wait()
            one = contract(x_in[i], weights_in[i, :, :both], 1, 0)
            two = contract(dy_in[i], weights_in[i, :, both:], 1, 0)
            pre = one if pre is None else pre + one
            back = two if back is None else back + two
        out[:, :both] = pre
        out[:, both:] = back

    weights = [w for _, w in first_parts] + [w for _, w in second_parts]
    shape = (slots, wide)
    return kernel_call(
        body,
        jax.ShapeDtypeStruct(shape, F32),
        60,
        in_specs=[far_memory()] * (1 + 2 * count),
        out_specs=whole(shape),
        scratch_shapes=[
            pltpu.VMEM((count, slots, part), BF16),
            pltpu.VMEM((count, slots, part), BF16),
            pltpu.VMEM((count, part, wide), BF16),
            pltpu.SemaphoreType.DMA((4, count)),
        ],
    )(rows, *weights)


def activations(rows, width, sums, first_part, second_part):
    count = rows.shape[0]
    far, first = first_part
    second = second_part[1]
    half, wide = first.shape
    part, units = 2 * half, wide // 3
    both = 2 * units

    def body(x_ref, dy_ref, prob_ref, sums_ref, first_ref, second_ref, acts_ref, prob_out):
        pre = sums_ref[:, :both] + contract(x_ref[:, :half], first_ref[:, :both], 1, 0)
        pre = pre + contract(x_ref[:, half:], second_ref[:, :both], 1, 0)
        back = sums_ref[:, both:] + contract(dy_ref[:, :half], first_ref[:, both:], 1, 0)
        back = back + contract(dy_ref[:, half:], second_ref[:, both:], 1, 0)
        gate_pre, up_pre = pre[:, :units], pre[:, units:]
        sigmoid_gate = jax.nn.sigmoid(gate_pre)
        hidden = (gate_pre * sigmoid_gate * up_pre).astype(BF16)
        prob_part = jnp.sum(hidden.astype(F32) * back, axis=1, keepdims=True)
        grad_hidden = prob_ref[:, :1].astype(F32) * back
        acts_ref[:, :units] = (
            grad_hidden * up_pre * sigmoid_gate * (1.0 + gate_pre * (1.0 - sigmoid_gate))
        ).astype(BF16)
        acts_ref[:, units:both] = (grad_hidden * gate_pre * sigmoid_gate).astype(BF16)
        acts_ref[:, both:] = hidden
        prob_out[...] = two_lanes(prob_part)

    acts_shape, prob_shape = (count, both + units), (count, LANES)
    return kernel_call(
        body,
        (jax.ShapeDtypeStruct(acts_shape, BF16), jax.ShapeDtypeStruct(prob_shape, BF16)),
        60,
        in_specs=[
            block_at((count, part), (0, far)),
            block_at((count, part), (0, width // part + far)),
            block_at((count, LANES), (0, 2 * width // LANES)),
            whole(sums.shape),
            whole(first.shape),
            whole(second.shape),
        ],
        out_specs=(whole(acts_shape), whole(prob_shape)),
    )(rows, rows, rows, sums, first, second)


def slot_sums(core, acts, prob_lanes, first_parts, second_parts):
    rows_half = acts.shape[0] // 2
    count = len(first_parts)
    half, wide = first_parts[0][1].shape
    part, both = 2 * half, wide // 3 * 2
    width = count * part
    first_parts = sorted(first_parts, key=lambda p: p[0])
    second_parts = sorted(second_parts, key=lambda p: p[0])

    def body(core_ref, acts_ref, prob_ref, *refs):
        weights, give, keep, weights_in, sems = refs[: 2 * count], *refs[2 * count :]
        copies = []
        for i in range(count):
            for k in range(2):
                copy = pltpu.make_async_copy(
                    weights[k * count + i].at[:, pl.ds(0, both)],
                    weights_in.at[i, pl.ds(k * half, half)],
                    sems.at[k, i],
                )
                copy.start()
                copies.append(copy)
        theirs = pl.ds(pl.multiple_of((1 - core_ref[0]) * rows_half, rows_half), rows_half)
        mine = pl.ds(pl.multiple_of(core_ref[0] * rows_half, rows_half), rows_half)
        acts = jnp.concatenate([acts_ref[theirs, :both], acts_ref[mine, :both]], axis=0)

        def step(i, carry):
            for k in range(2):
                rows = pl.ds(k * half, half)
                pltpu.make_async_copy(
                    weights[0].at[:, pl.ds(0, both)], weights_in.at[i, rows], sems.at[k, i]
                ).wait()
            sums = contract(acts, weights_in[i], 1, 1).astype(BF16)
            cols = pl.ds(pl.multiple_of(i * part, BLOCK), part)
            give[:, cols] = sums[:rows_half]
            keep[:, cols] = sums[rows_half:]
            return carry

        lax.fori_loop(0, count, step, 0)
        give[:, width:] = prob_ref[theirs, :]
        keep[:, width:] = prob_ref[mine, :]

    weights = [w for _, w in first_parts] + [w for _, w in second_parts]
    shape = (rows_half, width + LANES)
    return kernel_call(
        body,
        (jax.ShapeDtypeStruct(shape, BF16),) * 2,
        60,
        scalars=1,
        in_specs=[whole(acts.shape), whole(prob_lanes.shape)] + [far_memory()] * (2 * count),
        out_specs=(whole(shape),) * 2,
        scratch_shapes=[
            pltpu.VMEM((count, part, both), BF16),
            pltpu.SemaphoreType.DMA((2, count)),
        ],
    )(core, acts, prob_lanes, *weights)


def pair_sum(mine, other):
    width = mine.shape[1] - LANES

    def body(a_ref, b_ref, out):
        for at in range(0, width, 768):
            cols = slice(at, at + 768)
            out[:, cols] = (a_ref[:, cols].astype(F32) + b_ref[:, cols].astype(F32)).astype(BF16)
        lanes = a_ref[:, width:].astype(F32) + b_ref[:, width:].astype(F32)
        out[:, width:] = two_lanes(lanes[:, 0:1] + lanes[:, 1:2])

    return kernel_call(
        body,
        jax.ShapeDtypeStruct(mine.shape, BF16),
        16,
        in_specs=[whole(mine.shape)] * 2,
        out_specs=whole(mine.shape),
    )(mine, other)


def joined(packed, sides):
    ring, _, wide = sides.shape
    start = packed.shape[1]

    def body(packed_ref, sides_ref, out):
        out[:, :start] = packed_ref[...]
        for d in range(ring):
            out[:, start + d * wide : start + (d + 1) * wide] = sides_ref[d]

    shape = (CAP, start + ring * wide)
    return kernel_call(
        body,
        jax.ShapeDtypeStruct(shape, BF16),
        60,
        in_specs=[whole(packed.shape), whole(sides.shape)],
        out_specs=whole(shape),
    )(packed, sides)


def turned_columns(rows, start, part, ring):
    slots = rows.shape[0]

    def body(rows_ref, out, sides, sems):
        copies = [
            pltpu.make_async_copy(
                rows_ref.at[:, pl.ds(start + d * 2 * part, 2 * part)], sides.at[d], sems.at[d]
            )
            for d in range(ring)
        ]
        for copy in copies:
            copy.start()
        for d in range(ring):
            copies[d].wait()
            out[:, d * slots : (d + 1) * slots] = sides[d].astype(F32).T.astype(BF16)

    shape = (2 * part, ring * slots)
    return kernel_call(
        body,
        jax.ShapeDtypeStruct(shape, BF16),
        60,
        in_specs=[far_memory()],
        out_specs=whole(shape),
        scratch_shapes=[
            pltpu.VMEM((ring, slots, 2 * part), BF16),
            pltpu.SemaphoreType.DMA((ring,)),
        ],
    )(rows)


def weight_sums(columns, acts):
    twice, slots = columns.shape
    part = twice // 2
    wide = acts.shape[1]
    units = wide // 3
    both = 2 * units
    steps = 4
    span = slots // steps

    def body(columns_ref, acts_ref, gate_out, up_out, down_out, cols_in, acts_in, sums, sems):
        copies = []
        for i in range(steps):
            at = pl.ds(i * span, span)
            copies.append(
                (
                    pltpu.make_async_copy(acts_ref.at[at], acts_in.at[i], sems.at[0, i]),
                    pltpu.make_async_copy(columns_ref.at[:, at], cols_in.at[i], sems.at[1, i]),
                )
            )
            for copy in copies[-1]:
                copy.start()
        sums[...] = jnp.zeros_like(sums)

        def step(i, carry):
            at = pl.ds(0, span)
            pltpu.make_async_copy(acts_ref.at[at], acts_in.at[i], sems.at[0, i]).wait()
            pltpu.make_async_copy(columns_ref.at[:, at], cols_in.at[i], sems.at[1, i]).wait()
            sums[:, :both] += contract(cols_in[i, :part], acts_in[i, :, :both], 1, 0)
            sums[:, both:] += contract(cols_in[i, part:], acts_in[i, :, both:], 1, 0)
            return carry

        lax.fori_loop(0, steps, step, 0)
        gate_out[...] = sums[:, :units]
        up_out[...] = sums[:, units:both]
        down_out[...] = sums[:, both:].T

    shapes = ((part, units), (part, units), (units, part))
    return kernel_call(
        body,
        tuple(jax.ShapeDtypeStruct(v, F32) for v in shapes),
        60,
        in_specs=[far_memory()] * 2,
        out_specs=tuple(whole(v) for v in shapes),
        scratch_shapes=[
            pltpu.VMEM((steps, twice, span), BF16),
            pltpu.VMEM((steps, span, wide), BF16),
            pltpu.VMEM((part, wide), F32),
            pltpu.SemaphoreType.DMA((2, steps)),
        ],
    )(columns, acts)


def pick_slots(place, mask, prob, x_quant, x_scale, grad_out, ring):
    tokens, width = x_quant.shape
    part = width // ring

    def body(place_ref, mask_ref, prob_ref, x_ref, scale_ref, dy_ref, rows, sides, slot_out):
        mask = mask_ref[...]
        earlier = lax.broadcasted_iota(jnp.int32, (tokens, tokens), 0)
        later = lax.broadcasted_iota(jnp.int32, (tokens, tokens), 1)
        upto = (earlier <= later).astype(F32).astype(BF16)
        ones = jnp.broadcast_to(mask, (CAP, tokens)).astype(F32)
        rank = contract(ones.astype(BF16), upto, 1, 0) - 1.0
        wanted = lax.broadcasted_iota(jnp.int32, (CAP, tokens), 0).astype(F32)
        table = jnp.where((rank == wanted) & (ones == 1.0), 1.0, 0.0)
        slot_out[...] = jnp.where(mask == 1, rank[:1].astype(jnp.int32), -1)
        picked = table.astype(BF16)
        scale = lax.dot_general(
            table,
            scale_ref[...],
            (((1,), (1,)), ((), ())),
            precision=lax.Precision.HIGHEST,
            preferred_element_type=F32,
        )
        slot_prob = jnp.sum(table * prob_ref[...].astype(F32), axis=1, keepdims=True)
        for d in range(ring):
            cols = slice(d * part, (d + 1) * part)
            turned = ((place_ref[0] - d) & (ring - 1)) * part
            quant = contract(picked, x_ref[:, cols], 1, 0)
            x = jnp.concatenate(
                [
                    quant[:, k * BLOCK : (k + 1) * BLOCK]
                    * scale[:, d * part // BLOCK + k : d * part // BLOCK + k + 1]
                    for k in range(part // BLOCK)
                ],
                axis=1,
            ).astype(BF16)
            dy = contract(picked, dy_ref[:, cols], 1, 0)
            rows[:, pl.ds(pl.multiple_of(turned, BLOCK), part)] = x
            rows[:, pl.ds(pl.multiple_of(width + turned, BLOCK), part)] = dy.astype(BF16)
            sides[d, :, :part] = x
            sides[d, :, part:] = (slot_prob * dy).astype(BF16)
        rows[:, 2 * width :] = jnp.broadcast_to(slot_prob, (CAP, LANES)).astype(BF16)

    shapes = ((CAP, 2 * width + LANES), (ring, CAP, 2 * part), (1, tokens))
    inputs = [mask.reshape(1, tokens), prob.reshape(1, tokens), x_quant, x_scale.T, grad_out]
    return kernel_call(
        body,
        tuple(
            jax.ShapeDtypeStruct(v, t) for v, t in zip(shapes, (BF16, BF16, jnp.int32))
        ),
        60,
        scalars=1,
        in_specs=[whole(v.shape) for v in inputs],
        out_specs=tuple(whole(v) for v in shapes),
    )(place[None], *inputs)


def turn(values, axis, place, size):
    flipped = jnp.flip(values, axis)
    twice = jnp.concatenate([flipped, flipped], axis)
    return lax.dynamic_slice_in_dim(twice, size - 1 - place, size, axis)


def ring_gather(block, axis, size, last_up):
    up = [(i, (i + 1) % size) for i in range(size)]
    down = [(i, (i - 1) % size) for i in range(size)]
    far = size // 2
    parts = [(0, block)]
    ahead, behind = block, block
    for step in range(1, far):
        ahead = lax.ppermute(ahead, axis, up)
        behind = lax.ppermute(behind, axis, down)
        parts += [(step, ahead), (size - step, behind)]
    last = lax.ppermute(ahead, axis, up) if last_up else lax.ppermute(behind, axis, down)
    return parts, (far, last)


def make_on_device(mesh):
    ring = mesh.shape["fsdp"]

    def on_device(
        x_quant,
        x_scale,
        grad_out,
        route_mask,
        route_prob,
        gate_quant,
        gate_scale,
        up_quant,
        up_scale,
        down_quant,
        down_scale,
    ):
        place = lax.axis_index("fsdp")
        core = lax.axis_index("core")
        width = x_quant.shape[1]
        part = width // ring

        first, second = scaled_weights(
            gate_quant, gate_scale, up_quant, up_scale, down_quant, down_scale
        )
        first_near, first_far = ring_gather(first, "fsdp", ring, True)
        second_near, second_far = ring_gather(second, "fsdp", ring, False)

        packed, sides, token_slot = pick_slots(
            place, route_mask, route_prob, x_quant, x_scale, grad_out, ring
        )
        sides = lax.all_to_all(sides, "fsdp", split_axis=0, concat_axis=0, tiled=True)
        sides, *_ = lax.optimization_barrier((sides, *(w for _, w in first_near[1:3])))
        rows = lax.all_gather(joined(packed, sides), CORE_FIRST, axis=0, tiled=True)

        sums = pre_sums(rows, width, first_near, second_near)
        acts, prob_lanes = activations(rows, width, sums, first_far, second_far)
        all_acts = lax.all_gather(acts, "fsdp", axis=0, tiled=True)

        give, keep = slot_sums(
            core[None], acts, prob_lanes, [*first_near, first_far], [*second_near, second_far]
        )
        got = lax.ppermute(give, "core", [(0, 1), (1, 0)])
        both = pair_sum(keep, got).reshape(-1, CAP, width + LANES)
        shares = lax.all_to_all(both, PLANE, split_axis=0, concat_axis=0, tiled=True)
        grad_gate, grad_up, grad_down = weight_sums(
            turned_columns(rows, 2 * width + LANES, part, ring), all_acts
        )
        shares, grad_up = lax.optimization_barrier((shares, grad_up))
        table = token_slot == jnp.arange(CAP, dtype=jnp.int32)[:, None]
        mine = jnp.sum(shares.astype(F32), axis=0)
        mine_grad = mine[:, :width].astype(BF16).reshape(CAP, ring, part)
        mine_grad = turn(mine_grad, 1, place, ring).reshape(CAP, width)
        mine_prob = mine[:, width] + mine[:, width + 1]
        grad_x = contract(table.astype(BF16), mine_grad, 0, 0).astype(BF16)
        grad_prob = jnp.sum(jnp.where(table, mine_prob[:, None], 0.0), axis=0)

        return (grad_x, grad_prob, grad_gate, grad_up, grad_down)

    return on_device


def solution(mesh):
    devices = mesh.devices
    mesh = Mesh(devices.reshape(devices.shape[0], 4, 4, 2), ("fsdp", "x", "y", "core"))
    tokens = ("fsdp", "x", "y", "core")
    placed = (
        P(tokens, None),
        P(tokens, None),
        P(tokens, None),
        P(tokens),
        P(tokens),
        P("fsdp", EXPERT),
        P("fsdp", EXPERT),
        P("fsdp", EXPERT),
        P("fsdp", EXPERT),
        P(EXPERT, "fsdp"),
        P(EXPERT, "fsdp"),
    )
    return jax.shard_map(
        make_on_device(mesh),
        mesh=mesh,
        in_specs=placed,
        out_specs=(
            P(tokens, None),
            P(tokens),
            P("fsdp", EXPERT),
            P("fsdp", EXPERT),
            P(EXPERT, "fsdp"),
        ),
        check_vma=False,
    )
```

```python
import jax
import jax.numpy as jnp
from jax import lax
from jax.experimental import pallas as pl
from jax.experimental.pallas import tpu as pltpu
from jax.sharding import Mesh
from jax.sharding import PartitionSpec as P

CAP = 8
PLANE = ("x", "y")
EXPERT = ("x", "y", "core")
CORE_FIRST = ("core", "x", "y")
LANES = 128
BLOCK = 128
BF16 = jnp.bfloat16
F32 = jnp.float32


def contract(left, right, left_dim, right_dim):
    return lax.dot_general(
        left, right, (((left_dim,), (right_dim,)), ((), ())), preferred_element_type=F32
    )


def kernel_call(body, outs, limit, scalars=0, grid=(1,), **specs):
    grid_spec = pltpu.PrefetchScalarGridSpec(num_scalar_prefetch=scalars, grid=grid, **specs)
    return pl.pallas_call(
        body,
        out_shape=outs,
        grid_spec=grid_spec,
        compiler_params=pltpu.CompilerParams(vmem_limit_bytes=limit << 20),
    )


def far_memory():
    return pl.BlockSpec(memory_space=pl.ANY)


def whole(shape):
    return pl.BlockSpec(shape, lambda *_: (0,) * len(shape), pipeline_mode=pl.Buffered(1))


def block_at(shape, where):
    return pl.BlockSpec(shape, lambda *_: where, pipeline_mode=pl.Buffered(1))


def two_lanes(column):
    high = column.astype(BF16).astype(F32)
    lane = lax.broadcasted_iota(jnp.int32, (column.shape[0], LANES), 1)
    spread = jnp.where(lane == 0, high, jnp.where(lane == 1, column - high, 0.0))
    return spread.astype(BF16)


def scaled_weights(gate_quant, gate_scale, up_quant, up_scale, down_quant, down_scale):
    part, units = gate_quant.shape
    half = part // 2

    def body(gate, up, down, gate_s, up_s, down_s, first, second):
        for i in range(part // BLOCK):
            rows = slice(i * BLOCK, (i + 1) * BLOCK)
            out, at = (first, i * BLOCK) if i * BLOCK < half else (second, i * BLOCK - half)
            for j in range(units // BLOCK):
                cols = slice(j * BLOCK, (j + 1) * BLOCK)
                tiles = (
                    gate[rows, cols].astype(F32) * gate_s[j, i],
                    up[rows, cols].astype(F32) * up_s[j, i],
                    (down[cols, rows].astype(F32) * down_s[j, i]).T,
                )
                for k, tile in enumerate(tiles):
                    to = k * units + j * BLOCK
                    out[at : at + BLOCK, to : to + BLOCK] = tile.astype(BF16)

    quants, scales = [gate_quant, up_quant, down_quant], [gate_scale.T, up_scale.T, down_scale]
    shape = (half, 3 * units)
    return kernel_call(
        body,
        (jax.ShapeDtypeStruct(shape, BF16),) * 2,
        60,
        in_specs=[whole(v.shape) for v in quants] + [pl.BlockSpec(memory_space=pltpu.SMEM)] * 3,
        out_specs=(whole(shape),) * 2,
    )(*quants, *scales)


def pre_sums(rows, width, first_parts, second_parts):
    count = len(first_parts)
    half, wide = first_parts[0][1].shape
    part, both = 2 * half, wide // 3 * 2
    slots = rows.shape[0]
    places = [r for r, _ in first_parts]
    assert places == [r for r, _ in second_parts]

    def body(rows_ref, *refs):
        weights, out = refs[: 2 * count], refs[2 * count]
        x_in, dy_in, weights_in, sems = refs[2 * count + 1 :]
        copies = []
        for i, r in enumerate(places):
            pairs = (
                (rows_ref.at[:, pl.ds(r * part, part)], x_in.at[i]),
                (rows_ref.at[:, pl.ds(width + r * part, part)], dy_in.at[i]),
                (weights[i], weights_in.at[i, pl.ds(0, half)]),
                (weights[count + i], weights_in.at[i, pl.ds(half, half)]),
            )
            copies.append(
                [
                    pltpu.make_async_copy(source, into, sems.at[k, i])
                    for k, (source, into) in enumerate(pairs)
                ]
            )
            for copy in copies[-1]:
                copy.start()
        pre = back = None
        for i in range(count):
            for copy in copies[i]:
                copy.wait()
            one = contract(x_in[i], weights_in[i, :, :both], 1, 0)
            two = contract(dy_in[i], weights_in[i, :, both:], 1, 0)
            pre = one if pre is None else pre + one
            back = two if back is None else back + two
        out[:, :both] = pre
        out[:, both:] = back

    weights = [w for _, w in first_parts] + [w for _, w in second_parts]
    shape = (slots, wide)
    return kernel_call(
        body,
        jax.ShapeDtypeStruct(shape, F32),
        60,
        in_specs=[far_memory()] * (1 + 2 * count),
        out_specs=whole(shape),
        scratch_shapes=[
            pltpu.VMEM((count, slots, part), BF16),
            pltpu.VMEM((count, slots, part), BF16),
            pltpu.VMEM((count, part, wide), BF16),
            pltpu.SemaphoreType.DMA((4, count)),
        ],
    )(rows, *weights)


def activations(rows, width, sums, first_part, second_part):
    count = rows.shape[0]
    far, first = first_part
    second = second_part[1]
    half, wide = first.shape
    part, units = 2 * half, wide // 3
    both = 2 * units

    def body(x_ref, dy_ref, prob_ref, sums_ref, first_ref, second_ref, acts_ref, prob_out):
        pre = sums_ref[:, :both] + contract(x_ref[:, :half], first_ref[:, :both], 1, 0)
        pre = pre + contract(x_ref[:, half:], second_ref[:, :both], 1, 0)
        back = sums_ref[:, both:] + contract(dy_ref[:, :half], first_ref[:, both:], 1, 0)
        back = back + contract(dy_ref[:, half:], second_ref[:, both:], 1, 0)
        gate_pre, up_pre = pre[:, :units], pre[:, units:]
        sigmoid_gate = jax.nn.sigmoid(gate_pre)
        hidden = (gate_pre * sigmoid_gate * up_pre).astype(BF16)
        prob_part = jnp.sum(hidden.astype(F32) * back, axis=1, keepdims=True)
        grad_hidden = prob_ref[:, :1].astype(F32) * back
        acts_ref[:, :units] = (
            grad_hidden * up_pre * sigmoid_gate * (1.0 + gate_pre * (1.0 - sigmoid_gate))
        ).astype(BF16)
        acts_ref[:, units:both] = (grad_hidden * gate_pre * sigmoid_gate).astype(BF16)
        acts_ref[:, both:] = hidden
        prob_out[...] = two_lanes(prob_part)

    acts_shape, prob_shape = (count, both + units), (count, LANES)
    return kernel_call(
        body,
        (jax.ShapeDtypeStruct(acts_shape, BF16), jax.ShapeDtypeStruct(prob_shape, BF16)),
        60,
        in_specs=[
            block_at((count, part), (0, far)),
            block_at((count, part), (0, width // part + far)),
            block_at((count, LANES), (0, 2 * width // LANES)),
            whole(sums.shape),
            whole(first.shape),
            whole(second.shape),
        ],
        out_specs=(whole(acts_shape), whole(prob_shape)),
    )(rows, rows, rows, sums, first, second)


def slot_sums(whose, acts, prob_lanes, first_parts, second_parts):
    rows_half = acts.shape[0] // 2
    count = len(first_parts)
    half, wide = first_parts[0][1].shape
    part, both = 2 * half, wide // 3 * 2
    width = count * part
    first_parts = sorted(first_parts, key=lambda p: p[0])
    second_parts = sorted(second_parts, key=lambda p: p[0])

    def body(whose_ref, acts_ref, prob_ref, *refs):
        weights, out, weights_in, sems = refs[: 2 * count], *refs[2 * count :]
        copies = []
        for i in range(count):
            for k in range(2):
                copy = pltpu.make_async_copy(
                    weights[k * count + i].at[:, pl.ds(0, both)],
                    weights_in.at[i, pl.ds(k * half, half)],
                    sems.at[k, i],
                )
                copy.start()
                copies.append(copy)
        rows = pl.ds(pl.multiple_of(whose_ref[0] * rows_half, rows_half), rows_half)
        acts = acts_ref[rows, :both]

        def step(i, carry):
            for k in range(2):
                piece = pl.ds(k * half, half)
                pltpu.make_async_copy(
                    weights[0].at[:, pl.ds(0, both)], weights_in.at[i, piece], sems.at[k, i]
                ).wait()
            cols = pl.ds(pl.multiple_of(i * part, BLOCK), part)
            out[:, cols] = contract(acts, weights_in[i], 1, 1).astype(BF16)
            return carry

        lax.fori_loop(0, count, step, 0)
        out[:, width:] = prob_ref[rows, :]

    weights = [w for _, w in first_parts] + [w for _, w in second_parts]
    shape = (rows_half, width + LANES)
    return kernel_call(
        body,
        jax.ShapeDtypeStruct(shape, BF16),
        60,
        scalars=1,
        in_specs=[whole(acts.shape), whole(prob_lanes.shape)] + [far_memory()] * (2 * count),
        out_specs=whole(shape),
        scratch_shapes=[
            pltpu.VMEM((count, part, both), BF16),
            pltpu.SemaphoreType.DMA((2, count)),
        ],
    )(whose, acts, prob_lanes, *weights)


def pair_sum(mine, other):
    width = mine.shape[1] - LANES

    def body(a_ref, b_ref, out):
        for at in range(0, width, 768):
            cols = slice(at, at + 768)
            out[:, cols] = (a_ref[:, cols].astype(F32) + b_ref[:, cols].astype(F32)).astype(BF16)
        lanes = a_ref[:, width:].astype(F32) + b_ref[:, width:].astype(F32)
        out[:, width:] = two_lanes(lanes[:, 0:1] + lanes[:, 1:2])

    return kernel_call(
        body,
        jax.ShapeDtypeStruct(mine.shape, BF16),
        60,
        in_specs=[whole(mine.shape)] * 2,
        out_specs=whole(mine.shape),
    )(mine, other)


def joined(packed, sides):
    ring, _, wide = sides.shape
    start = packed.shape[1]

    def body(packed_ref, sides_ref, out):
        out[:, :start] = packed_ref[...]
        for d in range(ring):
            out[:, start + d * wide : start + (d + 1) * wide] = sides_ref[d]

    shape = (CAP, start + ring * wide)
    return kernel_call(
        body,
        jax.ShapeDtypeStruct(shape, BF16),
        60,
        in_specs=[whole(packed.shape), whole(sides.shape)],
        out_specs=whole(shape),
    )(packed, sides)


def turned_columns(rows, start, part, ring):
    slots = rows.shape[0]

    def body(rows_ref, out, sides, sems):
        copies = [
            pltpu.make_async_copy(
                rows_ref.at[:, pl.ds(start + d * 2 * part, 2 * part)], sides.at[d], sems.at[d]
            )
            for d in range(ring)
        ]
        for copy in copies:
            copy.start()
        for d in range(ring):
            copies[d].wait()
            out[:, d * slots : (d + 1) * slots] = sides[d].astype(F32).T.astype(BF16)

    shape = (2 * part, ring * slots)
    return kernel_call(
        body,
        jax.ShapeDtypeStruct(shape, BF16),
        60,
        in_specs=[far_memory()],
        out_specs=whole(shape),
        scratch_shapes=[
            pltpu.VMEM((ring, slots, 2 * part), BF16),
            pltpu.SemaphoreType.DMA((ring,)),
        ],
    )(rows)


def weight_sums(columns, acts):
    twice, slots = columns.shape
    part = twice // 2
    wide = acts.shape[1]
    units = wide // 3
    both = 2 * units
    steps = 4
    span = slots // steps

    def body(columns_ref, acts_ref, gate_out, up_out, down_out, cols_in, acts_in, sums, sems):
        copies = []
        for i in range(steps):
            at = pl.ds(i * span, span)
            copies.append(
                (
                    pltpu.make_async_copy(acts_ref.at[at], acts_in.at[i], sems.at[0, i]),
                    pltpu.make_async_copy(columns_ref.at[:, at], cols_in.at[i], sems.at[1, i]),
                )
            )
            for copy in copies[-1]:
                copy.start()
        sums[...] = jnp.zeros_like(sums)

        def step(i, carry):
            at = pl.ds(0, span)
            pltpu.make_async_copy(acts_ref.at[at], acts_in.at[i], sems.at[0, i]).wait()
            pltpu.make_async_copy(columns_ref.at[:, at], cols_in.at[i], sems.at[1, i]).wait()
            sums[:, :both] += contract(cols_in[i, :part], acts_in[i, :, :both], 1, 0)
            sums[:, both:] += contract(cols_in[i, part:], acts_in[i, :, both:], 1, 0)
            return carry

        lax.fori_loop(0, steps, step, 0)
        gate_out[...] = sums[:, :units]
        up_out[...] = sums[:, units:both]
        down_out[...] = sums[:, both:].T

    shapes = ((part, units), (part, units), (units, part))
    return kernel_call(
        body,
        tuple(jax.ShapeDtypeStruct(v, F32) for v in shapes),
        60,
        in_specs=[far_memory()] * 2,
        out_specs=tuple(whole(v) for v in shapes),
        scratch_shapes=[
            pltpu.VMEM((steps, twice, span), BF16),
            pltpu.VMEM((steps, span, wide), BF16),
            pltpu.VMEM((part, wide), F32),
            pltpu.SemaphoreType.DMA((2, steps)),
        ],
    )(columns, acts)


def pick_slots(place, mask, prob, x_quant, x_scale, grad_out, ring):
    tokens, width = x_quant.shape
    part = width // ring

    def body(place_ref, mask_ref, prob_ref, x_ref, scale_ref, dy_ref, rows, sides, slot_out):
        mask = mask_ref[...]
        earlier = lax.broadcasted_iota(jnp.int32, (tokens, tokens), 0)
        later = lax.broadcasted_iota(jnp.int32, (tokens, tokens), 1)
        upto = (earlier <= later).astype(F32).astype(BF16)
        ones = jnp.broadcast_to(mask, (CAP, tokens)).astype(F32)
        rank = contract(ones.astype(BF16), upto, 1, 0) - 1.0
        wanted = lax.broadcasted_iota(jnp.int32, (CAP, tokens), 0).astype(F32)
        table = jnp.where((rank == wanted) & (ones == 1.0), 1.0, 0.0)
        slot_out[...] = jnp.where(mask == 1, rank[:1].astype(jnp.int32), -1)
        picked = table.astype(BF16)
        scale = lax.dot_general(
            table,
            scale_ref[...],
            (((1,), (1,)), ((), ())),
            precision=lax.Precision.HIGHEST,
            preferred_element_type=F32,
        )
        slot_prob = jnp.sum(table * prob_ref[...].astype(F32), axis=1, keepdims=True)
        for d in range(ring):
            cols = slice(d * part, (d + 1) * part)
            turned = ((place_ref[0] - d) & (ring - 1)) * part
            quant = contract(picked, x_ref[:, cols], 1, 0)
            x = jnp.concatenate(
                [
                    quant[:, k * BLOCK : (k + 1) * BLOCK]
                    * scale[:, d * part // BLOCK + k : d * part // BLOCK + k + 1]
                    for k in range(part // BLOCK)
                ],
                axis=1,
            ).astype(BF16)
            dy = contract(picked, dy_ref[:, cols], 1, 0)
            rows[:, pl.ds(pl.multiple_of(turned, BLOCK), part)] = x
            rows[:, pl.ds(pl.multiple_of(width + turned, BLOCK), part)] = dy.astype(BF16)
            sides[d, :, :part] = x
            sides[d, :, part:] = (slot_prob * dy).astype(BF16)
        rows[:, 2 * width :] = jnp.broadcast_to(slot_prob, (CAP, LANES)).astype(BF16)

    shapes = ((CAP, 2 * width + LANES), (ring, CAP, 2 * part), (1, tokens))
    inputs = [mask.reshape(1, tokens), prob.reshape(1, tokens), x_quant, x_scale.T, grad_out]
    return kernel_call(
        body,
        tuple(
            jax.ShapeDtypeStruct(v, t) for v, t in zip(shapes, (BF16, BF16, jnp.int32))
        ),
        60,
        scalars=1,
        in_specs=[whole(v.shape) for v in inputs],
        out_specs=tuple(whole(v) for v in shapes),
    )(place[None], *inputs)


def turn(values, axis, place, size):
    flipped = jnp.flip(values, axis)
    twice = jnp.concatenate([flipped, flipped], axis)
    return lax.dynamic_slice_in_dim(twice, size - 1 - place, size, axis)


def ring_gather(block, axis, size, last_up):
    up = [(i, (i + 1) % size) for i in range(size)]
    down = [(i, (i - 1) % size) for i in range(size)]
    far = size // 2
    parts = [(0, block)]
    ahead, behind = block, block
    for step in range(1, far):
        ahead = lax.ppermute(ahead, axis, up)
        behind = lax.ppermute(behind, axis, down)
        parts += [(step, ahead), (size - step, behind)]
    last = lax.ppermute(ahead, axis, up) if last_up else lax.ppermute(behind, axis, down)
    return parts, (far, last)


def make_on_device(mesh):
    ring = mesh.shape["fsdp"]

    def on_device(
        x_quant,
        x_scale,
        grad_out,
        route_mask,
        route_prob,
        gate_quant,
        gate_scale,
        up_quant,
        up_scale,
        down_quant,
        down_scale,
    ):
        place = lax.axis_index("fsdp")
        core = lax.axis_index("core")
        width = x_quant.shape[1]
        part = width // ring

        first, second = scaled_weights(
            gate_quant, gate_scale, up_quant, up_scale, down_quant, down_scale
        )
        first_near, first_far = ring_gather(first, "fsdp", ring, True)
        second_near, second_far = ring_gather(second, "fsdp", ring, False)

        packed, sides, token_slot = pick_slots(
            place, route_mask, route_prob, x_quant, x_scale, grad_out, ring
        )
        sides = lax.all_to_all(sides, "fsdp", split_axis=0, concat_axis=0, tiled=True)
        sides, *_ = lax.optimization_barrier((sides, *(w for _, w in first_near[1:3])))
        rows = lax.all_gather(joined(packed, sides), CORE_FIRST, axis=0, tiled=True)

        sums = pre_sums(rows, width, first_near, second_near)
        acts, prob_lanes = activations(rows, width, sums, first_far, second_far)
        all_acts = lax.all_gather(acts, "fsdp", axis=0, tiled=True)

        sources = (acts, prob_lanes, [*first_near, first_far], [*second_near, second_far])
        give = slot_sums(1 - core[None], *sources)
        got = lax.ppermute(give, "core", [(0, 1), (1, 0)])
        keep = slot_sums(core[None], *sources)
        both = pair_sum(keep, got).reshape(-1, CAP, width + LANES)
        shares = lax.all_to_all(both, PLANE, split_axis=0, concat_axis=0, tiled=True)
        grad_gate, grad_up, grad_down = weight_sums(
            turned_columns(rows, 2 * width + LANES, part, ring), all_acts
        )
        table = token_slot == jnp.arange(CAP, dtype=jnp.int32)[:, None]
        mine = jnp.sum(shares.astype(F32), axis=0)
        mine_grad = mine[:, :width].astype(BF16).reshape(CAP, ring, part)
        mine_grad = turn(mine_grad, 1, place, ring).reshape(CAP, width)
        mine_prob = mine[:, width] + mine[:, width + 1]
        grad_x = contract(table.astype(BF16), mine_grad, 0, 0).astype(BF16)
        grad_prob = jnp.sum(jnp.where(table, mine_prob[:, None], 0.0), axis=0)

        return (grad_x, grad_prob, grad_gate, grad_up, grad_down)

    return on_device


def solution(mesh):
    devices = mesh.devices
    mesh = Mesh(devices.reshape(devices.shape[0], 4, 4, 2), ("fsdp", "x", "y", "core"))
    tokens = ("fsdp", "x", "y", "core")
    placed = (
        P(tokens, None),
        P(tokens, None),
        P(tokens, None),
        P(tokens),
        P(tokens),
        P("fsdp", EXPERT),
        P("fsdp", EXPERT),
        P("fsdp", EXPERT),
        P("fsdp", EXPERT),
        P(EXPERT, "fsdp"),
        P(EXPERT, "fsdp"),
    )
    return jax.shard_map(
        make_on_device(mesh),
        mesh=mesh,
        in_specs=placed,
        out_specs=(
            P(tokens, None),
            P(tokens),
            P("fsdp", EXPERT),
            P("fsdp", EXPERT),
            P(EXPERT, "fsdp"),
        ),
        check_vma=False,
    )
```
